32 devices in a mesh: groups: 2 (over y), req: 16 (over z, x, core).
Axes of the slice: x: 2, y: 2, z: 4, core: 2. Of those that a mesh axis runs over, the one named last changes fastest.
Arguments:
- kv_cache: bfloat16 [1152, 2, 128, 512], P(('groups', 'req')), parts along dimension 0
- draft_rows: bfloat16 [1536, 5120], P(('groups', 'req')), parts along dimension 0
- cache_lengths: int32 [384], P('groups'), parts along dimension 0, may hold values from 1 to 384, as said below
- row_offsets: int32 [32], P('groups'), parts along dimension 0, may hold values from 0 to 15, as said below
- draft_order: int32 [1536], P(('groups', 'req')), parts along dimension 0, may hold values from 0 to 47, as said below
- pair_mask: int32 [2], P('groups'), parts along dimension 0, may hold values from 1 to 15
- moved_slots: int32 [32], P('groups'), parts along dimension 0, may hold values from 0 to 11
Outputs:
- verified: bfloat16 [1536, 4096], P(('groups', 'req')), parts along dimension 0
The draws below stay inside these ranges and needn't reach their ends.
There are 2 independent parts, one for each index of `groups`. The reference program is written for one: setup_inputs(seed, part) draws one part's arguments, and reference() takes and returns one part's arrays. A program takes and returns all parts, laid end to end along the dimension named above; each array names one. Nothing has to cross between parts.
Inputs may be any that keep to these rules, and one draw needn't show every extreme that they name: `row_offsets`: all entries are different; the offsets 1, 15 and 8 are always among them. `draft_order`: each device's 48 entries are a permutation. `cache_lengths`: some request has exactly 384 positions.
All inputs are finite; a program needn't handle non-finite values.
Results may differ from the reference program's by a relative error of at most 0.0037.
Values may be sent and summed in bfloat16 or wider, within the bound.
A program may use at most 128 MiB of HBM per device.

```python
import jax
import jax.numpy as jnp
from jax import lax

QH = 32
KVH = 4
HD = 128
DRAFT = 4
PAGE = 128
R_DEV = 12
PPR = 3
LMAX = 384
QW = 4096
KVW = 512
ROW_W = 5120
DR_DEV = 48
CAP = 3
REQS = 192
ROWS = 768
CACHE_PAGES = 576
N_REQ = 16


def draw_kv_cache(key, part):
    values = jax.random.normal(jax.random.fold_in(key, 11), (CACHE_PAGES, 2, PAGE, KVH, HD), jnp.float32)
    return values.reshape(CACHE_PAGES, 2, PAGE, KVW).astype(jnp.bfloat16)


def draw_draft_rows(key, part):
    values = jax.random.normal(jax.random.fold_in(key, 21), (ROWS, ROW_W), jnp.float32)
    return values.astype(jnp.bfloat16)


def draw_cache_lengths(key, part):
    first = jax.random.randint(jax.random.fold_in(key, 31), (REQS,), 0, LMAX)
    second = jax.random.randint(jax.random.fold_in(key, 32), (REQS,), 0, LMAX)
    longest = jax.random.randint(jax.random.fold_in(key, 33), (), 0, REQS)
    lengths = 1 + first * second // LMAX
    return jnp.where(jnp.arange(REQS, dtype=jnp.int32) == longest, LMAX, lengths).astype(jnp.int32)


def draw_row_offsets(key, part):
    order = jax.random.permutation(jax.random.fold_in(key, 41), N_REQ).astype(jnp.int32)
    rank = jnp.argsort(order).astype(jnp.int32)
    values = jnp.arange(N_REQ, dtype=jnp.int32)
    forced = (values == 1) | (values == N_REQ - 1) | (values == N_REQ // 2)
    score = jnp.where(forced, rank - N_REQ, rank)
    chosen = jnp.argsort(score)[:DR_DEV // CAP].astype(jnp.int32)
    return jax.random.permutation(jax.random.fold_in(key, 42), chosen).astype(jnp.int32)


def draw_draft_order(key, part):
    subkeys = jax.random.split(jax.random.fold_in(key, 51), N_REQ)
    orders = jax.vmap(lambda sub: jax.random.permutation(sub, DR_DEV))(subkeys)
    return orders.reshape(ROWS).astype(jnp.int32)


def plant(drawn, rng, smallest, largest):
    longest = drawn.shape.index(max(drawn.shape))
    spots = []
    for shift in (0, 1):
        where = [jax.random.randint(jax.random.fold_in(rng, axis), (), 0, length) for axis, length in enumerate(drawn.shape)]
        where[longest] = (where[longest] + shift) % drawn.shape[longest]
        spots.append(tuple(where))
    return drawn.at[spots[0]].set(smallest).at[spots[1]].set(largest)


def setup_inputs(seed: int = 0, part: int = 0) -> dict:
    arg_keys = jax.random.split(jax.random.key(seed), 8)
    part_keys = jax.random.split(jax.random.fold_in(arg_keys[7], part), 8)
    kv_cache = draw_kv_cache(jax.random.fold_in(jax.random.fold_in(arg_keys[7], part), 71), part)
    draft_rows = draw_draft_rows(jax.random.fold_in(jax.random.fold_in(arg_keys[7], part), 71), part)
    cache_lengths = draw_cache_lengths(jax.random.fold_in(jax.random.fold_in(arg_keys[7], part), 71), part)
    row_offsets = draw_row_offsets(jax.random.fold_in(jax.random.fold_in(arg_keys[7], part), 71), part)
    draft_order = draw_draft_order(jax.random.fold_in(jax.random.fold_in(arg_keys[7], part), 71), part)
    pair_mask = jax.random.randint(part_keys[5], (1,), 1, N_REQ).astype(jnp.int32)
    moved_slots = plant(jax.random.randint(part_keys[6], (N_REQ,), 0, R_DEV), jax.random.fold_in(part_keys[6], 1), 0, R_DEV - 1).astype(jnp.int32)
    return {"kv_cache": kv_cache, "draft_rows": draft_rows, "cache_lengths": cache_lengths, "row_offsets": row_offsets, "draft_order": draft_order, "pair_mask": pair_mask, "moved_slots": moved_slots}


def attend_one(pages, length, row_block):
    grp = QH // KVH
    cache_keys = pages[:, 0].reshape(LMAX, KVH, HD).astype(jnp.float32)
    cache_vals = pages[:, 1].reshape(LMAX, KVH, HD).astype(jnp.float32)
    queries = row_block[:, :QW].reshape(DRAFT, KVH, grp, HD).astype(jnp.float32)
    new_keys = row_block[:, QW:QW + KVW].reshape(DRAFT, KVH, HD).astype(jnp.float32)
    new_vals = row_block[:, QW + KVW:].reshape(DRAFT, KVH, HD).astype(jnp.float32)
    factor = 1.0 / jnp.sqrt(jnp.float32(HD))
    cache_score = jnp.einsum('tghd,lgd->tghl', queries, cache_keys) * factor
    new_score = jnp.einsum('tghd,ugd->tghu', queries, new_keys) * factor
    cache_valid = (jnp.arange(LMAX, dtype=jnp.int32) < length)[None, None, None, :]
    positions = jnp.arange(DRAFT, dtype=jnp.int32)
    new_valid = (positions[None, :] <= positions[:, None])[:, None, None, :]
    cache_score = jnp.where(cache_valid, cache_score, jnp.float32(-1e+30))
    new_score = jnp.where(new_valid, new_score, jnp.float32(-1e+30))
    peak = jnp.maximum(lax.optimization_barrier(jnp.max(cache_score, axis=-1)), lax.optimization_barrier(jnp.max(new_score, axis=-1)))
    cache_weight = jnp.where(cache_valid, jnp.exp(cache_score - peak[..., None]), 0.0)
    new_weight = jnp.where(new_valid, jnp.exp(new_score - peak[..., None]), 0.0)
    denominator = lax.optimization_barrier(jnp.sum(cache_weight, axis=-1)) + lax.optimization_barrier(jnp.sum(new_weight, axis=-1))
    cache_weight = cache_weight.astype(jnp.bfloat16).astype(jnp.float32)
    new_weight = new_weight.astype(jnp.bfloat16).astype(jnp.float32)
    summed = jnp.einsum('tghl,lgd->tghd', cache_weight, cache_vals) + jnp.einsum('tghu,ugd->tghd', new_weight, new_vals)
    return (summed / denominator[..., None]).reshape(DRAFT, QW).astype(jnp.bfloat16)

def reference(kv_cache, draft_rows, cache_lengths, row_offsets, draft_order, pair_mask, moved_slots):
    page_pool = kv_cache.reshape(N_REQ, R_DEV, PPR, 2, PAGE, KVW)
    devices = jnp.arange(N_REQ, dtype=jnp.int32)
    partner = jnp.bitwise_xor(devices, pair_mask[0])
    slot_ids = jnp.arange(R_DEV, dtype=jnp.int32)
    moved_here = slot_ids[None, :] == moved_slots[:, None]
    ident_dev = jnp.where(moved_here, partner[:, None], devices[:, None])
    ident_slot = jnp.where(moved_here, moved_slots[partner][:, None], slot_ids[None, :])
    owner_k = draft_order.reshape(N_REQ, DR_DEV)
    owner_e = (devices[:, None] - row_offsets[owner_k // CAP]) % N_REQ
    owned = jnp.zeros((N_REQ, DR_DEV, ROW_W), jnp.bfloat16)
    owned = owned.at[owner_e.reshape(-1), owner_k.reshape(-1)].set(draft_rows)

    def per_owner(owner):

        def per_slot(slot):
            source_dev = ident_dev[owner, slot]
            source_slot = ident_slot[owner, slot]
            pages = page_pool[source_dev, source_slot]
            length = cache_lengths[source_dev * R_DEV + source_slot]
            row_block = lax.dynamic_slice_in_dim(owned[owner], slot * DRAFT, DRAFT, 0)
            return attend_one(pages, length, row_block)
        return lax.map(per_slot, slot_ids).reshape(DR_DEV, QW)
    owner_out = lax.map(per_owner, devices)
    verified = owner_out[owner_e.reshape(-1), owner_k.reshape(-1)]
    return verified
```

```python
import functools

import jax
import jax.numpy as jnp
from jax import lax
from jax.experimental import pallas as pl
from jax.experimental.pallas import tpu as pltpu
from jax.sharding import PartitionSpec as P

HD = 128
DRAFT = 4
PAGE = 128
R_DEV = 12
PPR = 3
QW = 4096
KVW = 512
GRP = 8
CHUNKS = 2
HEADS = QW // HD // CHUNKS
KV_HERE = KVW // HD // CHUNKS
PARTS = 5
PART_W = (QW + 2 * KVW) // CHUNKS // PARTS
Q_PARTS = HEADS * HD // PART_W
PART_HEADS = PART_W // HD
F32 = jnp.float32
BF16 = jnp.bfloat16
MESH = pl.DeviceIdType.MESH


def iota(shape, dim):
    return lax.broadcasted_iota(jnp.int32, shape, dim)


def small_div(x, c):
    return x if c == 1 else lax.shift_right_logical(x * (65536 // c + 1), 16)


def small_mod(x, c):
    return x - small_div(x, c) * c


def wrap(x, n):
    x = jnp.where(x < 0, x + n, x)
    return jnp.where(x >= n, x - n, x)


def lane_sum(hit, value):
    return jnp.sum(jnp.where(hit, value, 0).astype(F32), axis=1, keepdims=True).astype(jnp.int32)


def row_sum(hit, value):
    return jnp.sum(jnp.where(hit, value, 0).astype(F32), axis=0, keepdims=True).astype(jnp.int32)


def pick(columns, width):
    return (iota((columns.shape[0], width), 1) == columns).astype(F32).astype(BF16)


def dot(a, b):
    return jnp.dot(a, b, preferred_element_type=F32)


def dot_t(a, b):
    return lax.dot_general(a, b, (((1,), (1,)), ((), ())), preferred_element_type=F32)


def flip(device, delta):
    bit = 0
    out = device
    while delta >> bit:
        if (delta >> bit) & 1:
            out = out + (1 << bit) * (1 - 2 * ((device // (1 << bit)) % 2))
        bit += 1
    return out


def digits_of(n):
    bits = n.bit_length() - 1
    return [(b, 1 << min(2, bits - b)) for b in range(0, bits, 2)]


def kernel(
    n, cap, lengths, mask, moved, order_ref, off_ref, draft_ref, kv_hbm, out_ref,
    kv, send, recv, rows, res, back, home, xs, xr, ys, yr,
    kv_sem, send_sem, recv_sem, back_sem, home_sem, xs_sem, xr_sem, ys_sem, yr_sem,
):
    me = lax.axis_index("req")
    n_rows = order_ref.shape[1]
    block = send.shape[2]
    n_off = off_ref.shape[1]
    digits = digits_of(n)

    kv_copy = pltpu.make_async_copy(kv_hbm, kv, kv_sem)
    kv_copy.start()

    def peer_of(i):
        step = (i + n // 2 - 1) % (n - 1) + 1
        return (me + step) % n

    barrier = pltpu.get_barrier_semaphore()

    def greet(i, carry):
        pl.semaphore_signal(barrier, inc=1, device_id={"req": peer_of(i)}, device_id_type=MESH)
        return carry

    lax.fori_loop(0, n - 1, greet, 0)

    order = order_ref[...]
    off = off_ref[...]
    order_col = lane_sum(iota((n_rows, n_rows), 0) == iota((n_rows, n_rows), 1), order)
    off_of_row = lane_sum(iota((n_rows, n_off), 1) == small_div(order_col, cap), off)
    owner = wrap(me - off_of_row, n)
    place = small_mod(order_col, cap)
    wide = PARTS * n_rows
    col = iota((1, wide), 1)
    target = owner * block + place
    target = row_sum(iota((n_rows, wide), 0) == small_mod(col, n_rows), target)
    target = target + small_div(col, n_rows) * cap
    pack = (iota((n * block, wide), 0) == target).astype(F32).astype(BF16)

    def exchange(shape_send, shape_recv, s_sem, r_sem, c, peer):
        return pltpu.make_async_remote_copy(
            src_ref=shape_send.at[c, peer], dst_ref=shape_recv.at[c, me],
            send_sem=s_sem.at[c, peer], recv_sem=r_sem.at[c, me],
            device_id={"req": peer}, device_id_type=MESH,
        )

    def send_all(s_ref, r_ref, s_sem, r_sem, c):
        def body(i, carry):
            exchange(s_ref, r_ref, s_sem, r_sem, c, peer_of(i)).start()
            return carry

        lax.fori_loop(0, n - 1, body, 0)
        r_ref[c, me] = s_ref[c, me]

    def wait_recv(s_ref, r_ref, s_sem, r_sem, c):
        def body(i, carry):
            src = peer_of(i)
            pltpu.make_async_remote_copy(
                src_ref=s_ref.at[c, src], dst_ref=r_ref.at[c, src],
                send_sem=s_sem.at[c, src], recv_sem=r_sem.at[c, src],
                device_id={"req": src}, device_id_type=MESH,
            ).wait_recv()
            return carry

        lax.fori_loop(0, n - 1, body, 0)

    def wait_send(s_ref, r_ref, s_sem, r_sem, c):
        def body(i, carry):
            exchange(s_ref, r_ref, s_sem, r_sem, c, peer_of(i)).wait_send()
            return carry

        lax.fori_loop(0, n - 1, body, 0)

    for c in range(CHUNKS):
        q0 = c * HEADS * HD
        kw = KV_HERE * HD
        keys = draft_ref[:, QW + c * kw : QW + (c + 1) * kw]
        vals = draft_ref[:, QW + KVW + c * kw : QW + KVW + (c + 1) * kw]
        parts = [draft_ref[:, q0 + p * PART_W : q0 + (p + 1) * PART_W] for p in range(Q_PARTS)]
        stacked = jnp.concatenate(parts + [jnp.concatenate([keys, vals], axis=1)], axis=0)
        send[c] = dot(pack, stacked).astype(BF16).reshape(n, block, PART_W)
        if c == 0:
            pl.semaphore_wait(barrier, n - 1)
        send_all(send, recv, send_sem, recv_sem, c)

    my_slot = moved[me]
    pair = mask[0]
    r_col = iota((wide, 1), 0)
    k_col = small_mod(r_col, n_rows)
    off_col = lane_sum(iota((wide, n_off), 1) == small_div(k_col, cap), off)
    source = wrap(me + off_col, n)
    from_col = source * block + small_div(r_col, n_rows) * cap + small_mod(k_col, cap)
    is_moved = lax.shift_right_logical(k_col, 2) == my_slot
    unpack = pick(jnp.where(is_moved, -1, from_col), n * block)
    x_row = iota((4 * DRAFT, 1), 0)
    x_draft = small_mod(x_row, DRAFT)
    x_k = my_slot * DRAFT + x_draft
    x_off = lane_sum(iota((4 * DRAFT, n_off), 1) == small_div(x_k, cap), off)
    x_from = wrap(me + x_off, n) * block + small_mod(x_k, cap)
    x_tile = small_div(x_row, DRAFT)
    x_pick = pick(x_from + x_tile * cap, n * block)
    x_last = [pick(jnp.where(x_tile == i, x_from + Q_PARTS * cap, -1), n * block) for i in range(4)]
    q_rows = Q_PARTS * n_rows
    x_in = pick(
        jnp.where(is_moved, small_div(r_col, n_rows) * DRAFT + small_mod(k_col, DRAFT), -1)[:q_rows],
        4 * DRAFT,
    )
    last_moved = is_moved[q_rows:]
    last_draft = small_mod(k_col, DRAFT)[q_rows:]
    x_in_last = [pick(jnp.where(last_moved, i * DRAFT + last_draft, -1), 4 * DRAFT) for i in range(4)]
    flat = HEADS * n_rows
    y_row = iota((HEADS * DRAFT, 1), 0)
    y_pick = pick(
        small_div(y_row, DRAFT) * n_rows + my_slot * DRAFT + small_mod(y_row, DRAFT), flat
    )
    f_row = iota((flat, 1), 0)
    f_k = small_mod(f_row, n_rows)
    f_head = small_div(f_row, n_rows)
    f_moved = lax.shift_right_logical(f_k, 2) == my_slot
    y_in = pick(f_head * DRAFT + small_mod(f_k, DRAFT), HEADS * DRAFT)
    p_row = iota((n * HEADS, 1), 0)
    p_peer = small_div(p_row, HEADS)
    p_hit = p_peer == wrap(me + off, n)
    p_index = lane_sum(p_hit, iota((1, n_off), 1) + 1) - 1
    p_base = small_mod(p_row, HEADS) * n_rows + p_index * cap

    def swap(cur, s_ref, r_ref, s_sem, r_sem, c):
        slot = 0
        for shift, values in digits:
            s_ref[c, slot] = cur
            copies = []
            for delta in range(1, values):
                copies.append(
                    pltpu.make_async_remote_copy(
                        src_ref=s_ref.at[c, slot], dst_ref=r_ref.at[c, slot + delta - 1],
                        send_sem=s_sem.at[c, slot + delta - 1],
                        recv_sem=r_sem.at[c, slot + delta - 1],
                        device_id={"req": flip(me, delta << shift)}, device_id_type=MESH,
                    )
                )
                copies[-1].start()
            yield
            digit = jnp.bitwise_and(jnp.right_shift(pair, shift), values - 1)
            for delta in range(1, values):
                copies[delta - 1].wait()
                cur = jnp.where(digit == delta, r_ref[c, slot + delta - 1], cur)
            slot += values - 1
        return cur

    half = DRAFT
    rows_p = 2 * DRAFT
    span = PPR * PAGE
    factor = 1.0 / jnp.sqrt(F32(HD))
    block_row = small_mod(iota((GRP * rows_p, 1), 0), rows_p)
    first = block_row < half
    n_col = iota((GRP * rows_p, rows_p), 1)
    new_ok = (lax.shift_right_logical(n_col, 2) == lax.shift_right_logical(block_row, 2)) & (
        n_col <= block_row
    )
    position = iota((GRP * rows_p, span), 1)

    def attend(c):
        def body(pr, carry):
            at = pl.multiple_of(pr * rows_p, rows_p)
            slot = pr * 2
            limit = jnp.where(first, lengths[me * R_DEV + slot], lengths[me * R_DEV + slot + 1])
            ok = position < limit

            def cached(which, g):
                lanes = slice((c * KV_HERE + g) * HD, (c * KV_HERE + g + 1) * HD)
                return jnp.concatenate(
                    [kv[pl.ds((slot + a) * PPR, PPR), which, :, lanes].reshape(span, HD) for a in (0, 1)],
                    axis=1,
                )

            for g in range(KV_HERE):
                tiles = []
                for h in range(GRP):
                    p, i = divmod(g * GRP + h, PART_HEADS)
                    tiles.append(rows[c, pl.ds(p * n_rows + at, rows_p), i * HD : (i + 1) * HD])
                q = jnp.concatenate(tiles, axis=0)
                last = pl.ds(Q_PARTS * n_rows + at, rows_p)
                new_k = rows[c, last, g * HD : (g + 1) * HD].astype(BF16)
                new_v = rows[c, last, (KV_HERE + g) * HD : (KV_HERE + g + 1) * HD].astype(BF16)
                q2 = jnp.concatenate([jnp.where(first, q, 0.0), jnp.where(first, 0.0, q)], axis=1)
                score = dot_t(q2.astype(BF16), cached(0, g)) * factor
                new_score = dot_t(q.astype(BF16), new_k) * factor
                score = jnp.where(ok, score, -1e30)
                new_score = jnp.where(new_ok, new_score, -1e30)
                peak = jnp.maximum(
                    jnp.max(score, axis=1, keepdims=True), jnp.max(new_score, axis=1, keepdims=True)
                )
                w = jnp.where(ok, jnp.exp(score - peak), 0.0)
                new_w = jnp.where(new_ok, jnp.exp(new_score - peak), 0.0)
                total = jnp.sum(w, axis=1, keepdims=True) + jnp.sum(new_w, axis=1, keepdims=True)
                both = dot(w.astype(BF16), cached(1, g))
                out = jnp.where(first, both[:, :HD], both[:, HD:]) + dot(new_w.astype(BF16), new_v)
                out = (out / total).reshape(GRP, rows_p, HD)
                res[c, g * GRP : (g + 1) * GRP, pl.ds(at, rows_p), :] = out
            return carry

        lax.fori_loop(0, R_DEV // 2, body, 0)

    def work(c):
        wait_recv(send, recv, send_sem, recv_sem, c)
        got = recv[c].reshape(n * block, PART_W)
        last = sum(dot(x_last[i], got[:, i * HD : (i + 1) * HD]) for i in range(4))
        mine = jnp.concatenate([dot(x_pick, got), last], axis=1).astype(BF16)
        own = dot(unpack, got)
        visitor = yield from swap(mine, xs, xr, xs_sem, xr_sem, c)
        tail = visitor[:, PART_W:]
        added = jnp.concatenate(
            [dot(x_in, visitor[:, :PART_W]),
             jnp.concatenate([dot(m, tail) for m in x_in_last], axis=1)], axis=0
        )
        rows[c] = own + added
        if c == 0:
            kv_copy.wait()
        attend(c)
        flat_res = res[c].reshape(flat, HD).astype(BF16)
        answer = dot(y_pick, flat_res).astype(BF16)
        answer = yield from swap(answer, ys, yr, ys_sem, yr_sem, c)
        merged = jnp.where(f_moved, dot(y_in, answer), flat_res.astype(F32)).astype(BF16)
        for m in range(cap):
            chosen = pick(jnp.where(p_index < 0, -1, p_base + m), flat)
            back[c, :, :, m * HD : (m + 1) * HD] = (
                dot(chosen, merged).astype(BF16).reshape(n, HEADS, HD)
            )
        send_all(back, home, back_sem, home_sem, c)
        yield

    running = [work(c) for c in range(CHUNKS)]
    while running:
        for w in list(running):
            if next(w, running) is running:
                running.remove(w)

    j_hit = iota((flat, n_rows), 1) == f_k
    eye = iota((n_rows, n_rows), 0) == iota((n_rows, n_rows), 1)
    owner_row = row_sum(eye, owner)
    place_row = row_sum(eye, place)
    out_from = lane_sum(j_hit, owner_row) * HEADS + f_head
    out_place = lane_sum(j_hit, place_row)
    chosen = [pick(jnp.where(out_place == m, out_from, -1), n * HEADS) for m in range(cap)]
    for c in range(CHUNKS):
        wait_recv(back, home, back_sem, home_sem, c)
        got = home[c].reshape(n * HEADS, cap * HD)
        total = sum(dot(chosen[m], got[:, m * HD : (m + 1) * HD]) for m in range(cap)).astype(BF16)
        for h in range(HEADS):
            lanes = slice((c * HEADS + h) * HD, (c * HEADS + h + 1) * HD)
            out_ref[:, lanes] = total[h * n_rows : (h + 1) * n_rows]
    for c in range(CHUNKS):
        wait_send(send, recv, send_sem, recv_sem, c)
        wait_send(back, home, back_sem, home_sem, c)


def on_device(
    kv_cache, draft_rows, cache_lengths, row_offsets, draft_order, pair_mask, moved_slots
):
    n = lax.axis_size("req")
    n_rows = draft_rows.shape[0]
    cap = n_rows // row_offsets.shape[0]
    block = -(-PARTS * cap // 16) * 16
    swaps = sum(values - 1 for _, values in digits_of(n))
    x_shape = (CHUNKS, swaps, 4 * DRAFT, PART_W + HD)
    y_shape = (CHUNKS, swaps, HEADS * DRAFT, HD)
    vmem, smem = pltpu.VMEM, pltpu.SMEM
    dma = pltpu.SemaphoreType.DMA
    return pl.pallas_call(
        functools.partial(kernel, n, cap),
        out_shape=jax.ShapeDtypeStruct((n_rows, QW), BF16),
        in_specs=[pl.BlockSpec(memory_space=smem)] * 3
        + [pl.BlockSpec(memory_space=vmem)] * 3
        + [pl.BlockSpec(memory_space=pl.ANY)],
        out_specs=pl.BlockSpec(memory_space=vmem),
        scratch_shapes=[
            vmem(kv_cache.shape, BF16),
            vmem((CHUNKS, n, block, PART_W), BF16),
            vmem((CHUNKS, n, block, PART_W), BF16),
            vmem((CHUNKS, PARTS * n_rows, PART_W), F32),
            vmem((CHUNKS, HEADS, n_rows, HD), F32),
            vmem((CHUNKS, n, HEADS, cap * HD), BF16),
            vmem((CHUNKS, n, HEADS, cap * HD), BF16),
            vmem(x_shape, BF16),
            vmem(x_shape, BF16),
            vmem(y_shape, BF16),
            vmem(y_shape, BF16),
            dma,
            dma((CHUNKS, n)), dma((CHUNKS, n)), dma((CHUNKS, n)), dma((CHUNKS, n)),
            dma((CHUNKS, swaps)), dma((CHUNKS, swaps)), dma((CHUNKS, swaps)), dma((CHUNKS, swaps)),
        ],
        compiler_params=pltpu.CompilerParams(
            collective_id=0, has_side_effects=True, vmem_limit_bytes=56 * 1024 * 1024
        ),
    )(
        cache_lengths, pair_mask, moved_slots, draft_order.reshape(1, n_rows),
        row_offsets.reshape(1, row_offsets.shape[0]), draft_rows, kv_cache,
    )


def solution(mesh):
    in_specs = (
        P(("groups", "req"), None, None, None),
        P(("groups", "req"), None),
        P("groups"),
        P("groups"),
        P(("groups", "req")),
        P("groups"),
        P("groups"),
    )
    out_specs = P(("groups", "req"), None)
    return jax.shard_map(
        on_device, mesh=mesh, in_specs=in_specs, out_specs=out_specs, check_vma=False
    )
```

```python
import functools

import jax
import jax.numpy as jnp
from jax import lax
from jax.experimental import pallas as pl
from jax.experimental.pallas import tpu as pltpu
from jax.sharding import PartitionSpec as P

HD = 128
DRAFT = 4
PAGE = 128
R_DEV = 12
PPR = 3
QW = 4096
KVW = 512
GRP = 8
CHUNKS = 2
HEADS = QW // HD // CHUNKS
KV_HERE = KVW // HD // CHUNKS
PARTS = 5
PART_W = (QW + 2 * KVW) // CHUNKS // PARTS
Q_PARTS = HEADS * HD // PART_W
PART_HEADS = PART_W // HD
F32 = jnp.float32
BF16 = jnp.bfloat16
MESH = pl.DeviceIdType.MESH


def iota(shape, dim):
    return lax.broadcasted_iota(jnp.int32, shape, dim)


def small_div(x, c):
    return x if c == 1 else lax.shift_right_logical(x * (65536 // c + 1), 16)


def small_mod(x, c):
    return x - small_div(x, c) * c


def wrap(x, n):
    x = jnp.where(x < 0, x + n, x)
    return jnp.where(x >= n, x - n, x)


def lane_sum(hit, value):
    return jnp.sum(jnp.where(hit, value, 0).astype(F32), axis=1, keepdims=True).astype(jnp.int32)


def row_sum(hit, value):
    return jnp.sum(jnp.where(hit, value, 0).astype(F32), axis=0, keepdims=True).astype(jnp.int32)


def pick(columns, width):
    return (iota((columns.shape[0], width), 1) == columns).astype(F32).astype(BF16)


def dot(a, b):
    return jnp.dot(a, b, preferred_element_type=F32)


def dot_t(a, b):
    return lax.dot_general(a, b, (((1,), (1,)), ((), ())), preferred_element_type=F32)


def flip(device, delta):
    bit = 0
    out = device
    while delta >> bit:
        if (delta >> bit) & 1:
            out = out + (1 << bit) * (1 - 2 * ((device // (1 << bit)) % 2))
        bit += 1
    return out


def digits_of(n):
    bits = n.bit_length() - 1
    return [(b, 1 << min(2, bits - b)) for b in range(0, bits, 2)]


def kernel(
    n, cap, lengths, mask, moved, order_ref, off_ref, draft_ref, kv_hbm, out_ref,
    kv, send, recv, rows, res, partial, back, home, xs, xr, ys, yr,
    unpack, x_pick, back_pick, y_pick, out_pick,
    kv_sem, send_sem, recv_sem, back_sem, home_sem, xs_sem, xr_sem, ys_sem, yr_sem,
):
    me = lax.axis_index("req")
    n_rows = order_ref.shape[1]
    block = send.shape[2]
    n_off = off_ref.shape[1]
    digits = digits_of(n)

    kv_copy = pltpu.make_async_copy(kv_hbm, kv, kv_sem)
    kv_copy.start()

    def peer_of(i):
        step = (i + n // 2 - 1) % (n - 1) + 1
        return (me + step) % n

    barrier = pltpu.get_barrier_semaphore()

    def greet(i, carry):
        pl.semaphore_signal(barrier, inc=1, device_id={"req": peer_of(i)}, device_id_type=MESH)
        return carry

    lax.fori_loop(0, n - 1, greet, 0)

    order = order_ref[...]
    off = off_ref[...]
    order_col = lane_sum(iota((n_rows, n_rows), 0) == iota((n_rows, n_rows), 1), order)
    off_of_row = lane_sum(iota((n_rows, n_off), 1) == small_div(order_col, cap), off)
    owner = wrap(me - off_of_row, n)
    place = small_mod(order_col, cap)
    wide = PARTS * n_rows
    col = iota((1, wide), 1)
    target = owner * block + place
    target = row_sum(iota((n_rows, wide), 0) == small_mod(col, n_rows), target)
    target = target + small_div(col, n_rows) * cap
    pack = (iota((n * block, wide), 0) == target).astype(F32).astype(BF16)

    def exchange(shape_send, shape_recv, s_sem, r_sem, c, peer):
        return pltpu.make_async_remote_copy(
            src_ref=shape_send.at[c, peer], dst_ref=shape_recv.at[c, me],
            send_sem=s_sem.at[c, peer], recv_sem=r_sem.at[c, me],
            device_id={"req": peer}, device_id_type=MESH,
        )

    def send_all(s_ref, r_ref, s_sem, r_sem, c):
        def body(i, carry):
            exchange(s_ref, r_ref, s_sem, r_sem, c, peer_of(i)).start()
            return carry

        lax.fori_loop(0, n - 1, body, 0)
        r_ref[c, me] = s_ref[c, me]

    def wait_recv(s_ref, r_ref, s_sem, r_sem, c):
        def body(i, carry):
            src = peer_of(i)
            pltpu.make_async_remote_copy(
                src_ref=s_ref.at[c, src], dst_ref=r_ref.at[c, src],
                send_sem=s_sem.at[c, src], recv_sem=r_sem.at[c, src],
                device_id={"req": src}, device_id_type=MESH,
            ).wait_recv()
            return carry

        lax.fori_loop(0, n - 1, body, 0)

    def wait_send(s_ref, r_ref, s_sem, r_sem, c):
        def body(i, carry):
            exchange(s_ref, r_ref, s_sem, r_sem, c, peer_of(i)).wait_send()
            return carry

        lax.fori_loop(0, n - 1, body, 0)

    for c in range(CHUNKS):
        q0 = c * HEADS * HD
        kw = KV_HERE * HD
        keys = draft_ref[:, QW + c * kw : QW + (c + 1) * kw]
        vals = draft_ref[:, QW + KVW + c * kw : QW + KVW + (c + 1) * kw]
        parts = [draft_ref[:, q0 + p * PART_W : q0 + (p + 1) * PART_W] for p in range(Q_PARTS)]
        stacked = jnp.concatenate(parts + [jnp.concatenate([keys, vals], axis=1)], axis=0)
        send[c] = dot(pack, stacked).astype(BF16).reshape(n, block, PART_W)
        if c == 0:
            pl.semaphore_wait(barrier, n - 1)
        send_all(send, recv, send_sem, recv_sem, c)

    my_slot = moved[me]
    pair = mask[0]
    r_col = iota((wide, 1), 0)
    k_col = small_mod(r_col, n_rows)
    off_col = lane_sum(iota((wide, n_off), 1) == small_div(k_col, cap), off)
    source = wrap(me + off_col, n)
    from_col = source * block + small_div(r_col, n_rows) * cap + small_mod(k_col, cap)
    unpack[...] = pick(from_col, n * block)
    x_row = iota((4 * DRAFT, 1), 0)
    x_draft = small_mod(x_row, DRAFT)
    x_k = my_slot * DRAFT + x_draft
    x_off = lane_sum(iota((4 * DRAFT, n_off), 1) == small_div(x_k, cap), off)
    x_from = wrap(me + x_off, n) * block + small_mod(x_k, cap)
    x_tile = small_div(x_row, DRAFT)
    x_pick[:, : n * block] = pick(x_from + x_tile * cap, n * block)
    for i in range(4):
        x_pick[:, (1 + i) * n * block : (2 + i) * n * block] = pick(
            jnp.where(x_tile == i, x_from + Q_PARTS * cap, -1), n * block
        )
    flat = HEADS * n_rows
    p_row = iota((n * HEADS, 1), 0)
    p_peer = small_div(p_row, HEADS)
    p_head = small_mod(p_row, HEADS)
    p_index = lane_sum(p_peer == wrap(me + off, n), iota((1, n_off), 1) + 1) - 1
    y_base = (
        small_div(p_head, GRP) * GRP * DRAFT
        + small_mod(p_head, PART_HEADS) * 2 * DRAFT
        + small_mod(small_div(p_head, PART_HEADS), 2) * DRAFT
    )
    for m in range(cap):
        p_k = p_index * cap + m
        p_moved = lax.shift_right_arithmetic(p_k, 2) == my_slot
        stays = (p_index >= 0) & jnp.logical_not(p_moved)
        back_pick[m] = pick(jnp.where(stays, p_head * n_rows + p_k, -1), flat)
        y_pick[m] = pick(jnp.where(p_moved, y_base + p_k - my_slot * DRAFT, -1), HEADS * DRAFT)
    f_row = iota((flat, 1), 0)
    j_hit = iota((flat, n_rows), 1) == small_mod(f_row, n_rows)
    eye = iota((n_rows, n_rows), 0) == iota((n_rows, n_rows), 1)
    out_from = lane_sum(j_hit, row_sum(eye, owner)) * HEADS + small_div(f_row, n_rows)
    out_place = lane_sum(j_hit, row_sum(eye, place))
    for m in range(cap):
        out_pick[m] = pick(jnp.where(out_place == m, out_from, -1), n * HEADS)

    class Swap:
        def __init__(self, cur, s_ref, r_ref, s_sem, r_sem, c):
            self.cur, self.refs, self.c = cur, (s_ref, r_ref, s_sem, r_sem), c
            self.slot, self.todo = 0, list(digits)
            self.start()

        def start(self):
            s_ref, r_ref, s_sem, r_sem = self.refs
            shift, values = self.todo[0]
            c, slot = self.c, self.slot
            s_ref[c, slot] = self.cur
            self.copies = [
                pltpu.make_async_remote_copy(
                    src_ref=s_ref.at[c, slot], dst_ref=r_ref.at[c, slot + delta - 1],
                    send_sem=s_sem.at[c, slot + delta - 1],
                    recv_sem=r_sem.at[c, slot + delta - 1],
                    device_id={"req": flip(me, delta << shift)}, device_id_type=MESH,
                )
                for delta in range(1, values)
            ]
            for copy in self.copies:
                copy.start()

        def receive(self):
            r_ref = self.refs[1]
            shift, values = self.todo.pop(0)
            digit = jnp.bitwise_and(jnp.right_shift(pair, shift), values - 1)
            for delta in range(1, values):
                self.copies[delta - 1].wait()
                self.cur = jnp.where(digit == delta, r_ref[self.c, self.slot + delta - 1], self.cur)
            self.slot += values - 1

        def step(self):
            self.receive()
            if self.todo:
                self.start()

        def finish(self):
            while self.todo:
                self.step()
            return self.cur

    rows_p = 2 * DRAFT
    span = PPR * PAGE
    factor = 1.0 / jnp.sqrt(F32(HD))
    block_row = small_mod(iota((GRP * rows_p, 1), 0), rows_p)
    first = block_row < DRAFT
    n_col = iota((GRP * rows_p, rows_p), 1)
    new_ok = (lax.shift_right_logical(n_col, 2) == lax.shift_right_logical(block_row, 2)) & (
        n_col <= block_row
    )
    position = iota((GRP * rows_p, span), 1)

    def cached(slot, which, c, g):
        lanes = slice((c * KV_HERE + g) * HD, (c * KV_HERE + g + 1) * HD)
        return kv[pl.ds(slot * PPR, PPR), which, :, lanes].reshape(span, HD)

    def weigh(score, ok, new_score, new_ok):
        score = jnp.where(ok, score * factor, -1e30)
        new_score = jnp.where(new_ok, new_score * factor, -1e30)
        peak = jnp.maximum(
            jnp.max(score, axis=1, keepdims=True), jnp.max(new_score, axis=1, keepdims=True)
        )
        w = jnp.where(ok, jnp.exp(score - peak), 0.0)
        new_w = jnp.where(new_ok, jnp.exp(new_score - peak), 0.0)
        total = jnp.sum(w, axis=1, keepdims=True) + jnp.sum(new_w, axis=1, keepdims=True)
        return w.astype(BF16), new_w.astype(BF16), total

    def attend(c, g):
        for pr in range(R_DEV // 2):
            at = pr * rows_p
            slot = pr * 2
            limit = jnp.where(first, lengths[me * R_DEV + slot], lengths[me * R_DEV + slot + 1])
            both = [
                jnp.concatenate([cached(slot + a, which, c, g) for a in (0, 1)], axis=1)
                for which in (0, 1)
            ]
            tiles = []
            for h in range(GRP):
                p, i = divmod(g * GRP + h, PART_HEADS)
                r0 = p * n_rows + at
                tiles.append(rows[c, r0 : r0 + rows_p, i * HD : (i + 1) * HD])
            q = jnp.concatenate(tiles, axis=0)
            r0 = Q_PARTS * n_rows + at
            new_k = rows[c, r0 : r0 + rows_p, g * HD : (g + 1) * HD].astype(BF16)
            new_v = rows[c, r0 : r0 + rows_p, (KV_HERE + g) * HD : (KV_HERE + g + 1) * HD].astype(BF16)
            q2 = jnp.concatenate([jnp.where(first, q, 0.0), jnp.where(first, 0.0, q)], axis=1)
            w, new_w, total = weigh(
                dot_t(q2.astype(BF16), both[0]), position < limit, dot_t(q.astype(BF16), new_k), new_ok
            )
            out = dot(w, both[1])
            out = jnp.where(first, out[:, :HD], out[:, HD:]) + dot(new_w, new_v)
            res[c, g * GRP : (g + 1) * GRP, at : at + rows_p, :] = (out / total).reshape(
                GRP, rows_p, HD
            )

    v_rows = GRP * DRAFT
    v_row = iota((v_rows, 4 * DRAFT), 0)
    v_col = iota((v_rows, 4 * DRAFT), 1)
    v_position = iota((v_rows, span), 1)

    def attend_visitor(c, visitor):
        v = visitor.astype(F32)
        tail = v[:, PART_W:]
        new_k = tail.astype(BF16)
        new_v = jnp.concatenate([tail[2 * DRAFT :], tail[: 2 * DRAFT]], axis=0).astype(BF16)
        ok = v_position < lengths[me * R_DEV + my_slot]
        outs = []
        for g in range(KV_HERE):
            q = jnp.concatenate(
                [v[g * 2 * DRAFT : (g + 1) * 2 * DRAFT, i * HD : (i + 1) * HD] for i in range(PART_HEADS)],
                axis=0,
            ).astype(BF16)
            seen = (small_div(v_col, DRAFT) == g) & (small_mod(v_col, DRAFT) <= small_mod(v_row, DRAFT))
            w, new_w, total = weigh(
                dot_t(q, cached(my_slot, 0, c, g)), ok, dot_t(q, new_k), seen
            )
            outs.append((dot(w, cached(my_slot, 1, c, g)) + dot(new_w, new_v)) / total)
        return jnp.concatenate(outs, axis=0).astype(BF16)

    def arrive(c):
        wait_recv(send, recv, send_sem, recv_sem, c)
        got = recv[c].reshape(n * block, PART_W)
        stack = jnp.concatenate([got[:, i * HD : (i + 1) * HD] for i in range(4)], axis=0)
        mine = jnp.concatenate(
            [dot(x_pick[:, : n * block], got), dot(x_pick[:, n * block :], stack)], axis=1
        ).astype(BF16)
        x_swap = Swap(mine, xs, xr, xs_sem, xr_sem, c)
        rows[c] = dot(unpack[...], got)
        return x_swap

    def pack_back(c):
        flat_res = res[c].reshape(flat, HD).astype(BF16)
        for m in range(cap):
            partial[c, :, m * HD : (m + 1) * HD] = dot(back_pick[m], flat_res)

    def send_back(c, answer):
        for m in range(cap):
            lanes = slice(m * HD, (m + 1) * HD)
            total = partial[c, :, lanes] + dot(y_pick[m], answer)
            back[c, :, :, lanes] = total.astype(BF16).reshape(n, HEADS, HD)
        send_all(back, home, back_sem, home_sem, c)

    def finish(c):
        wait_recv(back, home, back_sem, home_sem, c)
        got = home[c].reshape(n * HEADS, cap * HD)
        total = sum(dot(out_pick[m], got[:, m * HD : (m + 1) * HD]) for m in range(cap)).astype(BF16)
        for h in range(HEADS):
            lanes = slice((c * HEADS + h) * HD, (c * HEADS + h + 1) * HD)
            out_ref[:, lanes] = total[h * n_rows : (h + 1) * n_rows]

    x0 = arrive(0)
    kv_copy.wait()
    attend(0, 0)
    x0.step()
    attend(0, 1)
    x1 = arrive(1)
    y0 = Swap(attend_visitor(0, x0.finish()), ys, yr, ys_sem, yr_sem, 0)
    attend(1, 0)
    x1.step()
    y0.step()
    attend(1, 1)
    pack_back(0)
    send_back(0, y0.finish())
    y1 = Swap(attend_visitor(1, x1.finish()), ys, yr, ys_sem, yr_sem, 1)
    pack_back(1)
    send_back(1, y1.finish())
    finish(0)
    finish(1)
    for c in range(CHUNKS):
        wait_send(send, recv, send_sem, recv_sem, c)
        wait_send(back, home, back_sem, home_sem, c)


def on_device(
    kv_cache, draft_rows, cache_lengths, row_offsets, draft_order, pair_mask, moved_slots
):
    n = lax.axis_size("req")
    n_rows = draft_rows.shape[0]
    cap = n_rows // row_offsets.shape[0]
    block = -(-PARTS * cap // 16) * 16
    swaps = sum(values - 1 for _, values in digits_of(n))
    x_shape = (CHUNKS, swaps, 4 * DRAFT, PART_W + HD)
    y_shape = (CHUNKS, swaps, HEADS * DRAFT, HD)
    vmem, smem = pltpu.VMEM, pltpu.SMEM
    dma = pltpu.SemaphoreType.DMA
    return pl.pallas_call(
        functools.partial(kernel, n, cap),
        out_shape=jax.ShapeDtypeStruct((n_rows, QW), BF16),
        in_specs=[pl.BlockSpec(memory_space=smem)] * 3
        + [pl.BlockSpec(memory_space=vmem)] * 3
        + [pl.BlockSpec(memory_space=pl.ANY)],
        out_specs=pl.BlockSpec(memory_space=vmem),
        scratch_shapes=[
            vmem(kv_cache.shape, BF16),
            vmem((CHUNKS, n, block, PART_W), BF16),
            vmem((CHUNKS, n, block, PART_W), BF16),
            vmem((CHUNKS, PARTS * n_rows, PART_W), F32),
            vmem((CHUNKS, HEADS, n_rows, HD), F32),
            vmem((CHUNKS, n * HEADS, cap * HD), F32),
            vmem((CHUNKS, n, HEADS, cap * HD), BF16),
            vmem((CHUNKS, n, HEADS, cap * HD), BF16),
            vmem(x_shape, BF16),
            vmem(x_shape, BF16),
            vmem(y_shape, BF16),
            vmem(y_shape, BF16),
            vmem((PARTS * n_rows, n * block), BF16),
            vmem((4 * DRAFT, 5 * n * block), BF16),
            vmem((cap, n * HEADS, HEADS * n_rows), BF16),
            vmem((cap, n * HEADS, HEADS * DRAFT), BF16),
            vmem((cap, HEADS * n_rows, n * HEADS), BF16),
            dma,
            dma((CHUNKS, n)), dma((CHUNKS, n)), dma((CHUNKS, n)), dma((CHUNKS, n)),
            dma((CHUNKS, swaps)), dma((CHUNKS, swaps)), dma((CHUNKS, swaps)), dma((CHUNKS, swaps)),
        ],
        compiler_params=pltpu.CompilerParams(
            collective_id=0, has_side_effects=True, vmem_limit_bytes=56 * 1024 * 1024
        ),
    )(
        cache_lengths, pair_mask, moved_slots, draft_order.reshape(1, n_rows),
        row_offsets.reshape(1, row_offsets.shape[0]), draft_rows, kv_cache,
    )


def solution(mesh):
    in_specs = (
        P(("groups", "req"), None, None, None),
        P(("groups", "req"), None),
        P("groups"),
        P("groups"),
        P(("groups", "req")),
        P("groups"),
        P("groups"),
    )
    out_specs = P(("groups", "req"), None)
    return jax.shard_map(
        on_device, mesh=mesh, in_specs=in_specs, out_specs=out_specs, check_vma=False
    )
```

```python
import functools

import jax
import jax.numpy as jnp
from jax import lax
from jax.experimental import pallas as pl
from jax.experimental.pallas import tpu as pltpu
from jax.sharding import PartitionSpec as P

HD = 128
DRAFT = 4
PAGE = 128
R_DEV = 12
PPR = 3
QW = 4096
KVW = 512
GRP = 8
CHUNKS = 2
HEADS = QW // HD // CHUNKS
KV_HERE = KVW // HD // CHUNKS
PARTS = 5
PART_W = (QW + 2 * KVW) // CHUNKS // PARTS
Q_PARTS = HEADS * HD // PART_W
PART_HEADS = PART_W // HD
F32 = jnp.float32
BF16 = jnp.bfloat16
MESH = pl.DeviceIdType.MESH


def iota(shape, dim):
    return lax.broadcasted_iota(jnp.int32, shape, dim)


def small_div(x, c):
    return x if c == 1 else lax.shift_right_logical(x * (65536 // c + 1), 16)


def small_mod(x, c):
    return x - small_div(x, c) * c


def wrap(x, n):
    x = jnp.where(x < 0, x + n, x)
    return jnp.where(x >= n, x - n, x)


def lane_sum(hit, value):
    return jnp.sum(jnp.where(hit, value, 0).astype(F32), axis=1, keepdims=True).astype(jnp.int32)


def row_sum(hit, value):
    return jnp.sum(jnp.where(hit, value, 0).astype(F32), axis=0, keepdims=True).astype(jnp.int32)


def pick(columns, width):
    return (iota((columns.shape[0], width), 1) == columns).astype(F32).astype(BF16)


def dot(a, b):
    return jnp.dot(a, b, preferred_element_type=F32)


def dot_t(a, b):
    return lax.dot_general(a, b, (((1,), (1,)), ((), ())), preferred_element_type=F32)


def flip(device, delta):
    bit = 0
    out = device
    while delta >> bit:
        if (delta >> bit) & 1:
            out = out + (1 << bit) * (1 - 2 * ((device // (1 << bit)) % 2))
        bit += 1
    return out


def digits_of(n):
    bits = n.bit_length() - 1
    return [(b, 1 << min(2, bits - b)) for b in range(0, bits, 2)]


def kernel(
    n, cap, lengths, mask, moved, order_ref, off_ref, draft_ref, kv_hbm, out_ref,
    kv, send, recv, rows, res, partial, back, home, xs, xr, ys, yr,
    unpack, x_pick, back_pick, y_pick, out_pick,
    kv_sem, send_sem, recv_sem, back_sem, home_sem, xs_sem, xr_sem, ys_sem, yr_sem,
):
    me = lax.axis_index("req")
    n_rows = order_ref.shape[1]
    block = send.shape[2]
    n_off = off_ref.shape[1]
    digits = digits_of(n)
    cuts = [1 + (n - 1) * i // 4 for i in (1, 2, 3)]

    kv_copy = pltpu.make_async_copy(kv_hbm, kv, kv_sem)
    kv_copy.start()

    bits = n.bit_length() - 1
    turn = [(1 << b) * (1 - 2 * ((me // (1 << b)) % 2)) for b in range(bits)]

    def each_peer(body, lo=1, hi=n):
        def one(i, carry):
            peer = me
            for b in range(bits):
                peer = peer + turn[b] * ((i // (1 << (bits - 1 - b))) % 2)
            body(peer)
            return carry

        if n <= 16:
            for i in range(lo, hi):
                one(i, 0)
        else:
            lax.fori_loop(lo, hi, one, 0)

    barrier = pltpu.get_barrier_semaphore()
    each_peer(
        lambda peer: pl.semaphore_signal(
            barrier, inc=1, device_id={"req": peer}, device_id_type=MESH
        )
    )

    order = order_ref[...]
    off = off_ref[...]
    order_col = lane_sum(iota((n_rows, n_rows), 0) == iota((n_rows, n_rows), 1), order)
    off_of_row = lane_sum(iota((n_rows, n_off), 1) == small_div(order_col, cap), off)
    owner = wrap(me - off_of_row, n)
    place = small_mod(order_col, cap)
    wide = PARTS * n_rows
    col = iota((1, wide), 1)
    target = owner * block + place
    target = row_sum(iota((n_rows, wide), 0) == small_mod(col, n_rows), target)
    target = target + small_div(col, n_rows) * cap
    pack = (iota((n * block, wide), 0) == target).astype(F32).astype(BF16)

    def exchange(shape_send, shape_recv, s_sem, r_sem, c, peer):
        return pltpu.make_async_remote_copy(
            src_ref=shape_send.at[c, peer], dst_ref=shape_recv.at[c, me],
            send_sem=s_sem.at[c, peer], recv_sem=r_sem.at[c, me],
            device_id={"req": peer}, device_id_type=MESH,
        )

    def send_some(s_ref, r_ref, s_sem, r_sem, c, lo, hi):
        each_peer(lambda peer: exchange(s_ref, r_ref, s_sem, r_sem, c, peer).start(), lo, hi)

    def wait_recv(s_ref, r_ref, s_sem, r_sem, c):
        each_peer(
            lambda src: pltpu.make_async_remote_copy(
                src_ref=s_ref.at[c, src], dst_ref=r_ref.at[c, src],
                send_sem=s_sem.at[c, src], recv_sem=r_sem.at[c, src],
                device_id={"req": src}, device_id_type=MESH,
            ).wait_recv()
        )

    def wait_send(s_ref, r_ref, s_sem, r_sem, c):
        each_peer(lambda peer: exchange(s_ref, r_ref, s_sem, r_sem, c, peer).wait_send())

    def send_rows(c, lo, hi):
        send_some(send, recv, send_sem, recv_sem, c, lo, hi)

    def send_answers(c, lo, hi):
        send_some(back, home, back_sem, home_sem, c, lo, hi)

    for c in range(CHUNKS):
        q0 = c * HEADS * HD
        kw = KV_HERE * HD
        keys = draft_ref[:, QW + c * kw : QW + (c + 1) * kw]
        vals = draft_ref[:, QW + KVW + c * kw : QW + KVW + (c + 1) * kw]
        parts = [draft_ref[:, q0 + p * PART_W : q0 + (p + 1) * PART_W] for p in range(Q_PARTS)]
        stacked = jnp.concatenate(parts + [jnp.concatenate([keys, vals], axis=1)], axis=0)
        send[c] = dot(pack, stacked).astype(BF16).reshape(n, block, PART_W)
        if c == 0:
            pl.semaphore_wait(barrier, n - 1)
            send_rows(0, 1, n)
        recv[c, me] = send[c, me]
    send_rows(1, 1, cuts[0])

    my_slot = moved[me]
    pair = mask[0]
    r_col = iota((wide, 1), 0)
    k_col = small_mod(r_col, n_rows)
    off_col = lane_sum(iota((wide, n_off), 1) == small_div(k_col, cap), off)
    source = wrap(me + off_col, n)
    from_col = source * block + small_div(r_col, n_rows) * cap + small_mod(k_col, cap)
    unpack[...] = pick(from_col, n * block)
    x_row = iota((4 * DRAFT, 1), 0)
    x_draft = small_mod(x_row, DRAFT)
    x_k = my_slot * DRAFT + x_draft
    x_off = lane_sum(iota((4 * DRAFT, n_off), 1) == small_div(x_k, cap), off)
    x_from = wrap(me + x_off, n) * block + small_mod(x_k, cap)
    x_tile = small_div(x_row, DRAFT)
    x_pick[:, : n * block] = pick(x_from + x_tile * cap, n * block)
    for i in range(4):
        x_pick[:, (1 + i) * n * block : (2 + i) * n * block] = pick(
            jnp.where(x_tile == i, x_from + Q_PARTS * cap, -1), n * block
        )
    flat = HEADS * n_rows
    p_row = iota((n * HEADS, 1), 0)
    p_peer = small_div(p_row, HEADS)
    p_head = small_mod(p_row, HEADS)
    p_index = lane_sum(p_peer == wrap(me + off, n), iota((1, n_off), 1) + 1) - 1
    y_base = (
        small_div(p_head, GRP) * GRP * DRAFT
        + small_mod(p_head, PART_HEADS) * 2 * DRAFT
        + small_mod(small_div(p_head, PART_HEADS), 2) * DRAFT
    )
    for m in range(cap):
        p_k = p_index * cap + m
        p_moved = lax.shift_right_arithmetic(p_k, 2) == my_slot
        stays = (p_index >= 0) & jnp.logical_not(p_moved)
        back_pick[m] = pick(jnp.where(stays, p_head * n_rows + p_k, -1), flat)
        y_pick[m] = pick(jnp.where(p_moved, y_base + p_k - my_slot * DRAFT, -1), HEADS * DRAFT)
    f_row = iota((flat, 1), 0)
    j_hit = iota((flat, n_rows), 1) == small_mod(f_row, n_rows)
    eye = iota((n_rows, n_rows), 0) == iota((n_rows, n_rows), 1)
    out_from = lane_sum(j_hit, row_sum(eye, owner)) * HEADS + small_div(f_row, n_rows)
    out_place = lane_sum(j_hit, row_sum(eye, place))
    for m in range(cap):
        out_pick[m] = pick(jnp.where(out_place == m, out_from, -1), n * HEADS)

    class Swap:
        def __init__(self, cur, s_ref, r_ref, s_sem, r_sem, c):
            self.cur, self.refs, self.c = cur, (s_ref, r_ref, s_sem, r_sem), c
            self.slot, self.todo = 0, list(digits)
            self.start()

        def start(self):
            s_ref, r_ref, s_sem, r_sem = self.refs
            shift, values = self.todo[0]
            c, slot = self.c, self.slot
            s_ref[c, slot] = self.cur
            self.copies = [
                pltpu.make_async_remote_copy(
                    src_ref=s_ref.at[c, slot], dst_ref=r_ref.at[c, slot + delta - 1],
                    send_sem=s_sem.at[c, slot + delta - 1],
                    recv_sem=r_sem.at[c, slot + delta - 1],
                    device_id={"req": flip(me, delta << shift)}, device_id_type=MESH,
                )
                for delta in range(1, values)
            ]
            for copy in self.copies:
                copy.start()

        def receive(self):
            r_ref = self.refs[1]
            shift, values = self.todo.pop(0)
            digit = jnp.bitwise_and(jnp.right_shift(pair, shift), values - 1)
            for delta in range(1, values):
                self.copies[delta - 1].wait()
                self.cur = jnp.where(digit == delta, r_ref[self.c, self.slot + delta - 1], self.cur)
            self.slot += values - 1

        def step(self):
            self.receive()
            if self.todo:
                self.start()

        def finish(self):
            while self.todo:
                self.step()
            return self.cur

    rows_p = 2 * DRAFT
    span = PPR * PAGE
    factor = 1.0 / jnp.sqrt(F32(HD))
    block_row = small_mod(iota((GRP * rows_p, 1), 0), rows_p)
    first = block_row < DRAFT
    n_col = iota((GRP * rows_p, rows_p), 1)
    new_ok = (lax.shift_right_logical(n_col, 2) == lax.shift_right_logical(block_row, 2)) & (
        n_col <= block_row
    )
    position = iota((GRP * rows_p, span), 1)

    def cached(slot, which, c, g):
        lanes = slice((c * KV_HERE + g) * HD, (c * KV_HERE + g + 1) * HD)
        return kv[pl.ds(slot * PPR, PPR), which, :, lanes].reshape(span, HD)

    def weigh(score, ok, new_score, new_ok):
        score = jnp.where(ok, score * factor, -1e30)
        new_score = jnp.where(new_ok, new_score * factor, -1e30)
        peak = jnp.maximum(
            jnp.max(score, axis=1, keepdims=True), jnp.max(new_score, axis=1, keepdims=True)
        )
        w = jnp.where(ok, jnp.exp(score - peak), 0.0)
        new_w = jnp.where(new_ok, jnp.exp(new_score - peak), 0.0)
        total = jnp.sum(w, axis=1, keepdims=True) + jnp.sum(new_w, axis=1, keepdims=True)
        return w.astype(BF16), new_w.astype(BF16), total

    def attend(c, g):
        for pr in range(R_DEV // 2):
            at = pr * rows_p
            slot = pr * 2
            limit = jnp.where(first, lengths[me * R_DEV + slot], lengths[me * R_DEV + slot + 1])
            both = [
                jnp.concatenate([cached(slot + a, which, c, g) for a in (0, 1)], axis=1)
                for which in (0, 1)
            ]
            tiles = []
            for h in range(GRP):
                p, i = divmod(g * GRP + h, PART_HEADS)
                r0 = p * n_rows + at
                tiles.append(rows[c, r0 : r0 + rows_p, i * HD : (i + 1) * HD])
            q = jnp.concatenate(tiles, axis=0)
            r0 = Q_PARTS * n_rows + at
            new_k = rows[c, r0 : r0 + rows_p, g * HD : (g + 1) * HD].astype(BF16)
            new_v = rows[c, r0 : r0 + rows_p, (KV_HERE + g) * HD : (KV_HERE + g + 1) * HD].astype(BF16)
            q2 = jnp.concatenate([jnp.where(first, q, 0.0), jnp.where(first, 0.0, q)], axis=1)
            w, new_w, total = weigh(
                dot_t(q2.astype(BF16), both[0]), position < limit, dot_t(q.astype(BF16), new_k), new_ok
            )
            out = dot(w, both[1])
            out = jnp.where(first, out[:, :HD], out[:, HD:]) + dot(new_w, new_v)
            res[c, g * GRP : (g + 1) * GRP, at : at + rows_p, :] = (out / total).reshape(
                GRP, rows_p, HD
            )

    v_rows = GRP * DRAFT
    v_row = iota((v_rows, 4 * DRAFT), 0)
    v_col = iota((v_rows, 4 * DRAFT), 1)
    v_position = iota((v_rows, span), 1)

    def attend_visitor(c, visitor):
        v = visitor.astype(F32)
        tail = v[:, PART_W:]
        new_k = tail.astype(BF16)
        new_v = jnp.concatenate([tail[2 * DRAFT :], tail[: 2 * DRAFT]], axis=0).astype(BF16)
        ok = v_position < lengths[me * R_DEV + my_slot]
        outs = []
        for g in range(KV_HERE):
            q = jnp.concatenate(
                [v[g * 2 * DRAFT : (g + 1) * 2 * DRAFT, i * HD : (i + 1) * HD] for i in range(PART_HEADS)],
                axis=0,
            ).astype(BF16)
            seen = (small_div(v_col, DRAFT) == g) & (small_mod(v_col, DRAFT) <= small_mod(v_row, DRAFT))
            w, new_w, total = weigh(
                dot_t(q, cached(my_slot, 0, c, g)), ok, dot_t(q, new_k), seen
            )
            outs.append((dot(w, cached(my_slot, 1, c, g)) + dot(new_w, new_v)) / total)
        return jnp.concatenate(outs, axis=0).astype(BF16)

    def arrive(c):
        wait_recv(send, recv, send_sem, recv_sem, c)
        got = recv[c].reshape(n * block, PART_W)
        stack = jnp.concatenate([got[:, i * HD : (i + 1) * HD] for i in range(4)], axis=0)
        mine = jnp.concatenate(
            [dot(x_pick[:, : n * block], got), dot(x_pick[:, n * block :], stack)], axis=1
        ).astype(BF16)
        x_swap = Swap(mine, xs, xr, xs_sem, xr_sem, c)
        rows[c] = dot(unpack[...], got)
        return x_swap

    def pack_back(c):
        flat_res = res[c].reshape(flat, HD).astype(BF16)
        for m in range(cap):
            partial[c, :, m * HD : (m + 1) * HD] = dot(back_pick[m], flat_res)

    def send_back(c, answer):
        for m in range(cap):
            lanes = slice(m * HD, (m + 1) * HD)
            total = partial[c, :, lanes] + dot(y_pick[m], answer)
            back[c, :, :, lanes] = total.astype(BF16).reshape(n, HEADS, HD)
        home[c, me] = back[c, me]

    def finish(c):
        wait_recv(back, home, back_sem, home_sem, c)
        got = home[c].reshape(n * HEADS, cap * HD)
        total = sum(dot(out_pick[m], got[:, m * HD : (m + 1) * HD]) for m in range(cap)).astype(BF16)
        for h in range(HEADS):
            out_ref[c * HEADS + h] = total[h * n_rows : (h + 1) * n_rows]

    x0 = arrive(0)
    send_rows(1, cuts[0], cuts[1])
    kv_copy.wait()
    attend(0, 0)
    x0.step()
    send_rows(1, cuts[1], cuts[2])
    attend(0, 1)
    y0 = Swap(attend_visitor(0, x0.finish()), ys, yr, ys_sem, yr_sem, 0)
    send_rows(1, cuts[2], n)
    pack_back(0)
    y0.step()
    x1 = arrive(1)
    attend(1, 0)
    x1.step()
    send_back(0, y0.finish())
    send_answers(0, 1, cuts[1])
    attend(1, 1)
    y1 = Swap(attend_visitor(1, x1.finish()), ys, yr, ys_sem, yr_sem, 1)
    send_answers(0, cuts[1], cuts[2])
    pack_back(1)
    y1.step()
    send_answers(0, cuts[2], n)
    send_back(1, y1.finish())
    send_answers(1, 1, n)
    finish(0)
    finish(1)
    for c in range(CHUNKS):
        wait_send(send, recv, send_sem, recv_sem, c)
        wait_send(back, home, back_sem, home_sem, c)


def on_device(
    kv_cache, draft_rows, cache_lengths, row_offsets, draft_order, pair_mask, moved_slots
):
    n = lax.axis_size("req")
    n_rows = draft_rows.shape[0]
    cap = n_rows // row_offsets.shape[0]
    block = -(-PARTS * cap // 16) * 16
    swaps = sum(values - 1 for _, values in digits_of(n))
    x_shape = (CHUNKS, swaps, 4 * DRAFT, PART_W + HD)
    y_shape = (CHUNKS, swaps, HEADS * DRAFT, HD)
    vmem, smem = pltpu.VMEM, pltpu.SMEM
    dma = pltpu.SemaphoreType.DMA
    heads_first = pl.pallas_call(
        functools.partial(kernel, n, cap),
        out_shape=jax.ShapeDtypeStruct((QW // HD, n_rows, HD), BF16),
        in_specs=[pl.BlockSpec(memory_space=smem)] * 3
        + [pl.BlockSpec(memory_space=vmem)] * 3
        + [pl.BlockSpec(memory_space=pl.ANY)],
        out_specs=pl.BlockSpec(memory_space=vmem),
        scratch_shapes=[
            vmem(kv_cache.shape, BF16),
            vmem((CHUNKS, n, block, PART_W), BF16),
            vmem((CHUNKS, n, block, PART_W), BF16),
            vmem((CHUNKS, PARTS * n_rows, PART_W), F32),
            vmem((CHUNKS, HEADS, n_rows, HD), F32),
            vmem((CHUNKS, n * HEADS, cap * HD), F32),
            vmem((CHUNKS, n, HEADS, cap * HD), BF16),
            vmem((CHUNKS, n, HEADS, cap * HD), BF16),
            vmem(x_shape, BF16),
            vmem(x_shape, BF16),
            vmem(y_shape, BF16),
            vmem(y_shape, BF16),
            vmem((PARTS * n_rows, n * block), BF16),
            vmem((4 * DRAFT, 5 * n * block), BF16),
            vmem((cap, n * HEADS, HEADS * n_rows), BF16),
            vmem((cap, n * HEADS, HEADS * DRAFT), BF16),
            vmem((cap, HEADS * n_rows, n * HEADS), BF16),
            dma,
            dma((CHUNKS, n)), dma((CHUNKS, n)), dma((CHUNKS, n)), dma((CHUNKS, n)),
            dma((CHUNKS, swaps)), dma((CHUNKS, swaps)), dma((CHUNKS, swaps)), dma((CHUNKS, swaps)),
        ],
        compiler_params=pltpu.CompilerParams(
            collective_id=0, has_side_effects=True, vmem_limit_bytes=56 * 1024 * 1024
        ),
    )(
        cache_lengths, pair_mask, moved_slots, draft_order.reshape(1, n_rows),
        row_offsets.reshape(1, row_offsets.shape[0]), draft_rows, kv_cache,
    )
    return heads_first.transpose(1, 0, 2).reshape(n_rows, QW)


def solution(mesh):
    in_specs = (
        P(("groups", "req"), None, None, None),
        P(("groups", "req"), None),
        P("groups"),
        P("groups"),
        P(("groups", "req")),
        P("groups"),
        P("groups"),
    )
    out_specs = P(("groups", "req"), None)
    return jax.shard_map(
        on_device, mesh=mesh, in_specs=in_specs, out_specs=out_specs, check_vma=False
    )
```

```python
import functools

import jax
import jax.numpy as jnp
from jax import lax
from jax.experimental import pallas as pl
from jax.experimental.pallas import tpu as pltpu
from jax.sharding import PartitionSpec as P

HD = 128
DRAFT = 4
PAGE = 128
R_DEV = 12
PPR = 3
QW = 4096
KVW = 512
GRP = 8
CHUNKS = 2
HEADS = QW // HD // CHUNKS
KV_HERE = KVW // HD // CHUNKS
PARTS = 5
PART_W = (QW + 2 * KVW) // CHUNKS // PARTS
Q_PARTS = HEADS * HD // PART_W
PART_HEADS = PART_W // HD
F32 = jnp.float32
BF16 = jnp.bfloat16
MESH = pl.DeviceIdType.MESH


def iota(shape, dim):
    return lax.broadcasted_iota(jnp.int32, shape, dim)


def small_div(x, c):
    return x if c == 1 else lax.shift_right_logical(x * (65536 // c + 1), 16)


def small_mod(x, c):
    return x - small_div(x, c) * c


def wrap(x, n):
    x = jnp.where(x < 0, x + n, x)
    return jnp.where(x >= n, x - n, x)


def lane_sum(hit, value):
    return jnp.sum(jnp.where(hit, value, 0).astype(F32), axis=1, keepdims=True).astype(jnp.int32)


def row_sum(hit, value):
    return jnp.sum(jnp.where(hit, value, 0).astype(F32), axis=0, keepdims=True).astype(jnp.int32)


def pick(columns, width):
    return (iota((columns.shape[0], width), 1) == columns).astype(F32).astype(BF16)


def dot(a, b):
    return jnp.dot(a, b, preferred_element_type=F32)


def dot_t(a, b):
    return lax.dot_general(a, b, (((1,), (1,)), ((), ())), preferred_element_type=F32)


def flip(device, delta):
    bit = 0
    out = device
    while delta >> bit:
        if (delta >> bit) & 1:
            out = out + (1 << bit) * (1 - 2 * ((device // (1 << bit)) % 2))
        bit += 1
    return out


def digits_of(n):
    bits = n.bit_length() - 1
    return [(0, 4)] + [(b, 2) for b in range(2, bits)]


def kernel(
    n, cap, lengths, mask, moved, order_ref, off_ref, draft_ref, kv_hbm, out_ref,
    kv, send, recv, rows, res, partial, back, home, xs, xr, ys, yr,
    unpack, x_pick, back_pick, y_pick, out_pick,
    kv_sem, send_sem, recv_sem, back_sem, home_sem, xs_sem, xr_sem, ys_sem, yr_sem,
):
    me = lax.axis_index("req")
    n_rows = order_ref.shape[1]
    block = send.shape[2]
    n_off = off_ref.shape[1]
    digits = digits_of(n)
    middle = n // 2

    kv_copy = pltpu.make_async_copy(kv_hbm, kv, kv_sem)
    kv_copy.start()

    bits = n.bit_length() - 1
    turn = [(1 << b) * (1 - 2 * ((me // (1 << b)) % 2)) for b in range(bits)]

    def each_peer(body, lo=1, hi=n):
        def one(i, carry):
            peer = me
            for b in range(bits):
                peer = peer + turn[b] * ((i // (1 << (bits - 1 - b))) % 2)
            body(peer)
            return carry

        if n <= 16:
            for i in range(lo, hi):
                one(i, 0)
        else:
            lax.fori_loop(lo, hi, one, 0)

    barrier = pltpu.get_barrier_semaphore()
    each_peer(
        lambda peer: pl.semaphore_signal(
            barrier, inc=1, device_id={"req": peer}, device_id_type=MESH
        )
    )

    order = order_ref[...]
    off = off_ref[...]
    order_col = lane_sum(iota((n_rows, n_rows), 0) == iota((n_rows, n_rows), 1), order)
    off_of_row = lane_sum(iota((n_rows, n_off), 1) == small_div(order_col, cap), off)
    owner = wrap(me - off_of_row, n)
    place = small_mod(order_col, cap)
    wide = PARTS * n_rows
    col = iota((1, wide), 1)
    target = owner * block + place
    target = row_sum(iota((n_rows, wide), 0) == small_mod(col, n_rows), target)
    target = target + small_div(col, n_rows) * cap
    pack = (iota((n * block, wide), 0) == target).astype(F32).astype(BF16)

    def exchange(shape_send, shape_recv, s_sem, r_sem, c, peer):
        return pltpu.make_async_remote_copy(
            src_ref=shape_send.at[c, peer], dst_ref=shape_recv.at[c, me],
            send_sem=s_sem.at[c, peer], recv_sem=r_sem.at[c, me],
            device_id={"req": peer}, device_id_type=MESH,
        )

    def send_some(s_ref, r_ref, s_sem, r_sem, c, lo, hi):
        each_peer(lambda peer: exchange(s_ref, r_ref, s_sem, r_sem, c, peer).start(), lo, hi)

    def wait_recv(s_ref, r_ref, s_sem, r_sem, c):
        each_peer(
            lambda src: pltpu.make_async_remote_copy(
                src_ref=s_ref.at[c, src], dst_ref=r_ref.at[c, src],
                send_sem=s_sem.at[c, src], recv_sem=r_sem.at[c, src],
                device_id={"req": src}, device_id_type=MESH,
            ).wait_recv()
        )

    def wait_send(s_ref, r_ref, s_sem, r_sem, c):
        each_peer(lambda peer: exchange(s_ref, r_ref, s_sem, r_sem, c, peer).wait_send())

    def send_rows(c, lo, hi):
        send_some(send, recv, send_sem, recv_sem, c, lo, hi)

    def send_answers(c, lo, hi):
        send_some(back, home, back_sem, home_sem, c, lo, hi)

    for c in range(CHUNKS):
        q0 = c * HEADS * HD
        kw = KV_HERE * HD
        keys = draft_ref[:, QW + c * kw : QW + (c + 1) * kw]
        vals = draft_ref[:, QW + KVW + c * kw : QW + KVW + (c + 1) * kw]
        parts = [draft_ref[:, q0 + p * PART_W : q0 + (p + 1) * PART_W] for p in range(Q_PARTS)]
        stacked = jnp.concatenate(parts + [jnp.concatenate([keys, vals], axis=1)], axis=0)
        send[c] = dot(pack, stacked).astype(BF16).reshape(n, block, PART_W)
        if c == 0:
            pl.semaphore_wait(barrier, n - 1)
        send_rows(c, 1, n)
        recv[c, me] = send[c, me]

    my_slot = moved[me]
    pair = mask[0]
    r_col = iota((wide, 1), 0)
    k_col = small_mod(r_col, n_rows)
    off_col = lane_sum(iota((wide, n_off), 1) == small_div(k_col, cap), off)
    source = wrap(me + off_col, n)
    from_col = source * block + small_div(r_col, n_rows) * cap + small_mod(k_col, cap)
    unpack[...] = pick(from_col, n * block)
    x_row = iota((4 * DRAFT, 1), 0)
    x_draft = small_mod(x_row, DRAFT)
    x_k = my_slot * DRAFT + x_draft
    x_off = lane_sum(iota((4 * DRAFT, n_off), 1) == small_div(x_k, cap), off)
    x_from = wrap(me + x_off, n) * block + small_mod(x_k, cap)
    x_tile = small_div(x_row, DRAFT)
    x_pick[:, : n * block] = pick(x_from + x_tile * cap, n * block)
    for i in range(4):
        x_pick[:, (1 + i) * n * block : (2 + i) * n * block] = pick(
            jnp.where(x_tile == i, x_from + Q_PARTS * cap, -1), n * block
        )
    flat = HEADS * n_rows
    p_row = iota((n * HEADS, 1), 0)
    p_peer = small_div(p_row, HEADS)
    p_head = small_mod(p_row, HEADS)
    p_index = lane_sum(p_peer == wrap(me + off, n), iota((1, n_off), 1) + 1) - 1
    y_base = (
        small_div(p_head, GRP) * GRP * DRAFT
        + small_mod(p_head, PART_HEADS) * 2 * DRAFT
        + small_mod(small_div(p_head, PART_HEADS), 2) * DRAFT
    )
    for m in range(cap):
        p_k = p_index * cap + m
        p_moved = lax.shift_right_arithmetic(p_k, 2) == my_slot
        stays = (p_index >= 0) & jnp.logical_not(p_moved)
        back_pick[m] = pick(jnp.where(stays, p_head * n_rows + p_k, -1), flat)
        y_pick[m] = pick(jnp.where(p_moved, y_base + p_k - my_slot * DRAFT, -1), HEADS * DRAFT)
    f_row = iota((flat, 1), 0)
    j_hit = iota((flat, n_rows), 1) == small_mod(f_row, n_rows)
    eye = iota((n_rows, n_rows), 0) == iota((n_rows, n_rows), 1)
    out_from = lane_sum(j_hit, row_sum(eye, owner)) * HEADS + small_div(f_row, n_rows)
    out_place = lane_sum(j_hit, row_sum(eye, place))
    for m in range(cap):
        out_pick[m] = pick(jnp.where(out_place == m, out_from, -1), n * HEADS)

    class Swap:
        def __init__(self, cur, s_ref, r_ref, s_sem, r_sem, c):
            self.cur, self.refs, self.c = cur, (s_ref, r_ref, s_sem, r_sem), c
            self.slot, self.todo = 0, list(digits)
            self.start()

        def start(self):
            s_ref, r_ref, s_sem, r_sem = self.refs
            shift, values = self.todo[0]
            c, slot = self.c, self.slot
            s_ref[c, slot] = self.cur
            self.copies = [
                pltpu.make_async_remote_copy(
                    src_ref=s_ref.at[c, slot], dst_ref=r_ref.at[c, slot + delta - 1],
                    send_sem=s_sem.at[c, slot + delta - 1],
                    recv_sem=r_sem.at[c, slot + delta - 1],
                    device_id={"req": flip(me, delta << shift)}, device_id_type=MESH,
                )
                for delta in range(1, values)
            ]
            for copy in self.copies:
                copy.start()

        def receive(self):
            r_ref = self.refs[1]
            shift, values = self.todo.pop(0)
            digit = jnp.bitwise_and(jnp.right_shift(pair, shift), values - 1)
            for delta in range(1, values):
                self.copies[delta - 1].wait()
                self.cur = jnp.where(digit == delta, r_ref[self.c, self.slot + delta - 1], self.cur)
            self.slot += values - 1

        def step(self):
            self.receive()
            if self.todo:
                self.start()

        def finish(self):
            while self.todo:
                self.step()
            return self.cur

    rows_p = 2 * DRAFT
    span = PPR * PAGE
    factor = 1.0 / jnp.sqrt(F32(HD))
    block_row = small_mod(iota((GRP * rows_p, 1), 0), rows_p)
    first = block_row < DRAFT
    n_col = iota((GRP * rows_p, rows_p), 1)
    new_ok = (lax.shift_right_logical(n_col, 2) == lax.shift_right_logical(block_row, 2)) & (
        n_col <= block_row
    )
    position = iota((GRP * rows_p, span), 1)

    def cached(slot, which, c, g):
        lanes = slice((c * KV_HERE + g) * HD, (c * KV_HERE + g + 1) * HD)
        return kv[pl.ds(slot * PPR, PPR), which, :, lanes].reshape(span, HD)

    def weigh(score, ok, new_score, new_ok):
        score = jnp.where(ok, score * factor, -1e30)
        new_score = jnp.where(new_ok, new_score * factor, -1e30)
        peak = jnp.maximum(
            jnp.max(score, axis=1, keepdims=True), jnp.max(new_score, axis=1, keepdims=True)
        )
        w = jnp.where(ok, jnp.exp(score - peak), 0.0)
        new_w = jnp.where(new_ok, jnp.exp(new_score - peak), 0.0)
        total = jnp.sum(w, axis=1, keepdims=True) + jnp.sum(new_w, axis=1, keepdims=True)
        return w.astype(BF16), new_w.astype(BF16), total

    def attend(c, g):
        for pr in range(R_DEV // 2):
            at = pr * rows_p
            slot = pr * 2
            limit = jnp.where(first, lengths[me * R_DEV + slot], lengths[me * R_DEV + slot + 1])
            both = [
                jnp.concatenate([cached(slot + a, which, c, g) for a in (0, 1)], axis=1)
                for which in (0, 1)
            ]
            tiles = []
            for h in range(GRP):
                p, i = divmod(g * GRP + h, PART_HEADS)
                r0 = p * n_rows + at
                tiles.append(rows[c, r0 : r0 + rows_p, i * HD : (i + 1) * HD])
            q = jnp.concatenate(tiles, axis=0)
            r0 = Q_PARTS * n_rows + at
            new_k = rows[c, r0 : r0 + rows_p, g * HD : (g + 1) * HD].astype(BF16)
            new_v = rows[c, r0 : r0 + rows_p, (KV_HERE + g) * HD : (KV_HERE + g + 1) * HD].astype(BF16)
            q2 = jnp.concatenate([jnp.where(first, q, 0.0), jnp.where(first, 0.0, q)], axis=1)
            w, new_w, total = weigh(
                dot_t(q2.astype(BF16), both[0]), position < limit, dot_t(q.astype(BF16), new_k), new_ok
            )
            out = dot(w, both[1])
            out = jnp.where(first, out[:, :HD], out[:, HD:]) + dot(new_w, new_v)
            res[c, g * GRP : (g + 1) * GRP, at : at + rows_p, :] = (out / total).reshape(
                GRP, rows_p, HD
            )

    v_rows = GRP * DRAFT
    v_row = iota((v_rows, 4 * DRAFT), 0)
    v_col = iota((v_rows, 4 * DRAFT), 1)
    v_position = iota((v_rows, span), 1)

    def attend_visitor(c, visitor):
        v = visitor.astype(F32)
        tail = v[:, PART_W:]
        new_k = tail.astype(BF16)
        new_v = jnp.concatenate([tail[2 * DRAFT :], tail[: 2 * DRAFT]], axis=0).astype(BF16)
        ok = v_position < lengths[me * R_DEV + my_slot]
        outs = []
        for g in range(KV_HERE):
            q = jnp.concatenate(
                [v[g * 2 * DRAFT : (g + 1) * 2 * DRAFT, i * HD : (i + 1) * HD] for i in range(PART_HEADS)],
                axis=0,
            ).astype(BF16)
            seen = (small_div(v_col, DRAFT) == g) & (small_mod(v_col, DRAFT) <= small_mod(v_row, DRAFT))
            w, new_w, total = weigh(
                dot_t(q, cached(my_slot, 0, c, g)), ok, dot_t(q, new_k), seen
            )
            outs.append((dot(w, cached(my_slot, 1, c, g)) + dot(new_w, new_v)) / total)
        return jnp.concatenate(outs, axis=0).astype(BF16)

    def arrive(c):
        wait_recv(send, recv, send_sem, recv_sem, c)
        got = recv[c].reshape(n * block, PART_W)
        stack = jnp.concatenate([got[:, i * HD : (i + 1) * HD] for i in range(4)], axis=0)
        mine = jnp.concatenate(
            [dot(x_pick[:, : n * block], got), dot(x_pick[:, n * block :], stack)], axis=1
        ).astype(BF16)
        x_swap = Swap(mine, xs, xr, xs_sem, xr_sem, c)
        rows[c] = dot(unpack[...], got)
        return x_swap

    def pack_back(c):
        flat_res = res[c].reshape(flat, HD).astype(BF16)
        for m in range(cap):
            partial[c, :, m * HD : (m + 1) * HD] = dot(back_pick[m], flat_res)

    def send_back(c, answer):
        for m in range(cap):
            lanes = slice(m * HD, (m + 1) * HD)
            total = partial[c, :, lanes] + dot(y_pick[m], answer)
            back[c, :, :, lanes] = total.astype(BF16).reshape(n, HEADS, HD)
        home[c, me] = back[c, me]

    def finish(c):
        wait_recv(back, home, back_sem, home_sem, c)
        got = home[c].reshape(n * HEADS, cap * HD)
        total = sum(dot(out_pick[m], got[:, m * HD : (m + 1) * HD]) for m in range(cap)).astype(BF16)
        for h in range(HEADS):
            out_ref[c * HEADS + h] = total[h * n_rows : (h + 1) * n_rows]

    x0 = arrive(0)
    kv_copy.wait()
    attend(0, 0)
    x0.step()
    attend(0, 1)
    x0.step()
    x1 = arrive(1)
    y0 = Swap(attend_visitor(0, x0.finish()), ys, yr, ys_sem, yr_sem, 0)
    attend(1, 0)
    x1.step()
    y0.step()
    attend(1, 1)
    x1.step()
    y0.step()
    pack_back(0)
    send_back(0, y0.finish())
    send_answers(0, 1, middle)
    y1 = Swap(attend_visitor(1, x1.finish()), ys, yr, ys_sem, yr_sem, 1)
    pack_back(1)
    y1.step()
    send_answers(0, middle, n)
    send_back(1, y1.finish())
    send_answers(1, 1, n)
    finish(0)
    finish(1)
    for c in range(CHUNKS):
        wait_send(send, recv, send_sem, recv_sem, c)
        wait_send(back, home, back_sem, home_sem, c)


def on_device(
    kv_cache, draft_rows, cache_lengths, row_offsets, draft_order, pair_mask, moved_slots
):
    n = lax.axis_size("req")
    n_rows = draft_rows.shape[0]
    cap = n_rows // row_offsets.shape[0]
    block = -(-PARTS * cap // 16) * 16
    swaps = sum(values - 1 for _, values in digits_of(n))
    x_shape = (CHUNKS, swaps, 4 * DRAFT, PART_W + HD)
    y_shape = (CHUNKS, swaps, HEADS * DRAFT, HD)
    vmem, smem = pltpu.VMEM, pltpu.SMEM
    dma = pltpu.SemaphoreType.DMA
    heads_first = pl.pallas_call(
        functools.partial(kernel, n, cap),
        out_shape=jax.ShapeDtypeStruct((QW // HD, n_rows, HD), BF16),
        in_specs=[pl.BlockSpec(memory_space=smem)] * 3
        + [pl.BlockSpec(memory_space=vmem)] * 3
        + [pl.BlockSpec(memory_space=pl.ANY)],
        out_specs=pl.BlockSpec(memory_space=vmem),
        scratch_shapes=[
            vmem(kv_cache.shape, BF16),
            vmem((CHUNKS, n, block, PART_W), BF16),
            vmem((CHUNKS, n, block, PART_W), BF16),
            vmem((CHUNKS, PARTS * n_rows, PART_W), F32),
            vmem((CHUNKS, HEADS, n_rows, HD), F32),
            vmem((CHUNKS, n * HEADS, cap * HD), F32),
            vmem((CHUNKS, n, HEADS, cap * HD), BF16),
            vmem((CHUNKS, n, HEADS, cap * HD), BF16),
            vmem(x_shape, BF16),
            vmem(x_shape, BF16),
            vmem(y_shape, BF16),
            vmem(y_shape, BF16),
            vmem((PARTS * n_rows, n * block), BF16),
            vmem((4 * DRAFT, 5 * n * block), BF16),
            vmem((cap, n * HEADS, HEADS * n_rows), BF16),
            vmem((cap, n * HEADS, HEADS * DRAFT), BF16),
            vmem((cap, HEADS * n_rows, n * HEADS), BF16),
            dma,
            dma((CHUNKS, n)), dma((CHUNKS, n)), dma((CHUNKS, n)), dma((CHUNKS, n)),
            dma((CHUNKS, swaps)), dma((CHUNKS, swaps)), dma((CHUNKS, swaps)), dma((CHUNKS, swaps)),
        ],
        compiler_params=pltpu.CompilerParams(
            collective_id=0, has_side_effects=True, vmem_limit_bytes=56 * 1024 * 1024
        ),
    )(
        cache_lengths, pair_mask, moved_slots, draft_order.reshape(1, n_rows),
        row_offsets.reshape(1, row_offsets.shape[0]), draft_rows, kv_cache,
    )
    return heads_first.transpose(1, 0, 2).reshape(n_rows, QW)


def solution(mesh):
    in_specs = (
        P(("groups", "req"), None, None, None),
        P(("groups", "req"), None),
        P("groups"),
        P("groups"),
        P(("groups", "req")),
        P("groups"),
        P("groups"),
    )
    out_specs = P(("groups", "req"), None)
    return jax.shard_map(
        on_device, mesh=mesh, in_specs=in_specs, out_specs=out_specs, check_vma=False
    )
```

```python
import functools

import jax
import jax.numpy as jnp
from jax import lax
from jax.experimental import pallas as pl
from jax.experimental.pallas import tpu as pltpu
from jax.sharding import PartitionSpec as P

HD = 128
DRAFT = 4
PAGE = 128
R_DEV = 12
PPR = 3
QW = 4096
KVW = 512
GRP = 8
CHUNKS = 2
HEADS = QW // HD // CHUNKS
KV_HERE = KVW // HD // CHUNKS
PARTS = 5
PART_W = (QW + 2 * KVW) // CHUNKS // PARTS
Q_PARTS = HEADS * HD // PART_W
PART_HEADS = PART_W // HD
F32 = jnp.float32
BF16 = jnp.bfloat16
MESH = pl.DeviceIdType.MESH


def iota(shape, dim):
    return lax.broadcasted_iota(jnp.int32, shape, dim)


def small_div(x, c):
    return x if c == 1 else lax.shift_right_logical(x * (65536 // c + 1), 16)


def small_mod(x, c):
    return x - small_div(x, c) * c


def wrap(x, n):
    x = jnp.where(x < 0, x + n, x)
    return jnp.where(x >= n, x - n, x)


def lane_sum(hit, value):
    return jnp.sum(jnp.where(hit, value, 0).astype(F32), axis=1, keepdims=True).astype(jnp.int32)


def row_sum(hit, value):
    return jnp.sum(jnp.where(hit, value, 0).astype(F32), axis=0, keepdims=True).astype(jnp.int32)


def pick(columns, width):
    return (iota((columns.shape[0], width), 1) == columns).astype(F32).astype(BF16)


def dot(a, b):
    return jnp.dot(a, b, preferred_element_type=F32)


def dot_t(a, b):
    return lax.dot_general(a, b, (((1,), (1,)), ((), ())), preferred_element_type=F32)


def flip(device, delta):
    bit = 0
    out = device
    while delta >> bit:
        if (delta >> bit) & 1:
            out = out + (1 << bit) * (1 - 2 * ((device // (1 << bit)) % 2))
        bit += 1
    return out


def digits_of(n):
    bits = n.bit_length() - 1
    return [(b, 1 << min(2, bits - b)) for b in range(0, bits, 2)]


def kernel(
    n, cap, lengths, mask, moved, order_ref, off_ref, draft_ref, kv_hbm, out_ref,
    kv, send, recv, rows, res, partial, back, home, xs, xr, ys, yr,
    unpack, x_pick, back_pick, y_pick, out_pick,
    kv_sem, send_sem, recv_sem, back_sem, home_sem, xs_sem, xr_sem, ys_sem, yr_sem,
):
    me = lax.axis_index("req")
    n_rows = order_ref.shape[1]
    block = send.shape[2]
    n_off = off_ref.shape[1]
    digits = digits_of(n)

    kv_copy = pltpu.make_async_copy(kv_hbm, kv, kv_sem)
    kv_copy.start()

    def peer_of(i):
        step = (i + n // 2 - 1) % (n - 1) + 1
        return (me + step) % n

    barrier = pltpu.get_barrier_semaphore()

    def greet(i, carry):
        pl.semaphore_signal(barrier, inc=1, device_id={"req": peer_of(i)}, device_id_type=MESH)
        return carry

    lax.fori_loop(0, n - 1, greet, 0)

    order = order_ref[...]
    off = off_ref[...]
    order_col = lane_sum(iota((n_rows, n_rows), 0) == iota((n_rows, n_rows), 1), order)
    off_of_row = lane_sum(iota((n_rows, n_off), 1) == small_div(order_col, cap), off)
    owner = wrap(me - off_of_row, n)
    place = small_mod(order_col, cap)
    wide = PARTS * n_rows
    col = iota((1, wide), 1)
    target = owner * block + place
    target = row_sum(iota((n_rows, wide), 0) == small_mod(col, n_rows), target)
    target = target + small_div(col, n_rows) * cap
    pack = (iota((n * block, wide), 0) == target).astype(F32).astype(BF16)

    def exchange(shape_send, shape_recv, s_sem, r_sem, c, peer):
        return pltpu.make_async_remote_copy(
            src_ref=shape_send.at[c, peer], dst_ref=shape_recv.at[c, me],
            send_sem=s_sem.at[c, peer], recv_sem=r_sem.at[c, me],
            device_id={"req": peer}, device_id_type=MESH,
        )

    def send_all(s_ref, r_ref, s_sem, r_sem, c):
        def body(i, carry):
            exchange(s_ref, r_ref, s_sem, r_sem, c, peer_of(i)).start()
            return carry

        lax.fori_loop(0, n - 1, body, 0)
        r_ref[c, me] = s_ref[c, me]

    def wait_recv(s_ref, r_ref, s_sem, r_sem, c):
        def body(i, carry):
            src = peer_of(i)
            pltpu.make_async_remote_copy(
                src_ref=s_ref.at[c, src], dst_ref=r_ref.at[c, src],
                send_sem=s_sem.at[c, src], recv_sem=r_sem.at[c, src],
                device_id={"req": src}, device_id_type=MESH,
            ).wait_recv()
            return carry

        lax.fori_loop(0, n - 1, body, 0)

    def wait_send(s_ref, r_ref, s_sem, r_sem, c):
        def body(i, carry):
            exchange(s_ref, r_ref, s_sem, r_sem, c, peer_of(i)).wait_send()
            return carry

        lax.fori_loop(0, n - 1, body, 0)

    for c in range(CHUNKS):
        q0 = c * HEADS * HD
        kw = KV_HERE * HD
        keys = draft_ref[:, QW + c * kw : QW + (c + 1) * kw]
        vals = draft_ref[:, QW + KVW + c * kw : QW + KVW + (c + 1) * kw]
        parts = [draft_ref[:, q0 + p * PART_W : q0 + (p + 1) * PART_W] for p in range(Q_PARTS)]
        stacked = jnp.concatenate(parts + [jnp.concatenate([keys, vals], axis=1)], axis=0)
        send[c] = dot(pack, stacked).astype(BF16).reshape(n, block, PART_W)
        if c == 0:
            pl.semaphore_wait(barrier, n - 1)
        send_all(send, recv, send_sem, recv_sem, c)

    my_slot = moved[me]
    pair = mask[0]
    r_col = iota((wide, 1), 0)
    k_col = small_mod(r_col, n_rows)
    off_col = lane_sum(iota((wide, n_off), 1) == small_div(k_col, cap), off)
    source = wrap(me + off_col, n)
    from_col = source * block + small_div(r_col, n_rows) * cap + small_mod(k_col, cap)
    unpack[...] = pick(from_col, n * block)
    x_row = iota((4 * DRAFT, 1), 0)
    x_draft = small_mod(x_row, DRAFT)
    x_k = my_slot * DRAFT + x_draft
    x_off = lane_sum(iota((4 * DRAFT, n_off), 1) == small_div(x_k, cap), off)
    x_from = wrap(me + x_off, n) * block + small_mod(x_k, cap)
    x_tile = small_div(x_row, DRAFT)
    x_pick[:, : n * block] = pick(x_from + x_tile * cap, n * block)
    for i in range(4):
        x_pick[:, (1 + i) * n * block : (2 + i) * n * block] = pick(
            jnp.where(x_tile == i, x_from + Q_PARTS * cap, -1), n * block
        )
    flat = HEADS * n_rows
    p_row = iota((n * HEADS, 1), 0)
    p_peer = small_div(p_row, HEADS)
    p_head = small_mod(p_row, HEADS)
    p_index = lane_sum(p_peer == wrap(me + off, n), iota((1, n_off), 1) + 1) - 1
    y_base = (
        small_div(p_head, GRP) * GRP * DRAFT
        + small_mod(p_head, PART_HEADS) * 2 * DRAFT
        + small_mod(small_div(p_head, PART_HEADS), 2) * DRAFT
    )
    for m in range(cap):
        p_k = p_index * cap + m
        p_moved = lax.shift_right_arithmetic(p_k, 2) == my_slot
        stays = (p_index >= 0) & jnp.logical_not(p_moved)
        back_pick[m] = pick(jnp.where(stays, p_head * n_rows + p_k, -1), flat)
        y_pick[m] = pick(jnp.where(p_moved, y_base + p_k - my_slot * DRAFT, -1), HEADS * DRAFT)
    f_row = iota((flat, 1), 0)
    j_hit = iota((flat, n_rows), 1) == small_mod(f_row, n_rows)
    eye = iota((n_rows, n_rows), 0) == iota((n_rows, n_rows), 1)
    out_from = lane_sum(j_hit, row_sum(eye, owner)) * HEADS + small_div(f_row, n_rows)
    out_place = lane_sum(j_hit, row_sum(eye, place))
    for m in range(cap):
        out_pick[m] = pick(jnp.where(out_place == m, out_from, -1), n * HEADS)

    class Swap:
        def __init__(self, parts, s_ref, r_ref, s_sem, r_sem):
            self.cur = jnp.concatenate(parts, axis=0)
            self.refs = (s_ref, r_ref, s_sem, r_sem)
            self.slot, self.todo = 0, list(digits)
            self.start()

        def start(self):
            s_ref, r_ref, s_sem, r_sem = self.refs
            shift, values = self.todo[0]
            slot = self.slot
            s_ref[slot] = self.cur
            self.copies = [
                pltpu.make_async_remote_copy(
                    src_ref=s_ref.at[slot], dst_ref=r_ref.at[slot + delta - 1],
                    send_sem=s_sem.at[slot + delta - 1],
                    recv_sem=r_sem.at[slot + delta - 1],
                    device_id={"req": flip(me, delta << shift)}, device_id_type=MESH,
                )
                for delta in range(1, values)
            ]
            for copy in self.copies:
                copy.start()

        def receive(self):
            r_ref = self.refs[1]
            shift, values = self.todo.pop(0)
            digit = jnp.bitwise_and(jnp.right_shift(pair, shift), values - 1)
            for delta in range(1, values):
                self.copies[delta - 1].wait()
                self.cur = jnp.where(digit == delta, r_ref[self.slot + delta - 1], self.cur)
            self.slot += values - 1

        def step(self):
            self.receive()
            if self.todo:
                self.start()

        def finish(self):
            while self.todo:
                self.step()
            rows = self.cur.shape[0] // CHUNKS
            return [self.cur[c * rows : (c + 1) * rows] for c in range(CHUNKS)]

    rows_p = 2 * DRAFT
    span = PPR * PAGE
    factor = 1.0 / jnp.sqrt(F32(HD))
    block_row = small_mod(iota((GRP * rows_p, 1), 0), rows_p)
    first = block_row < DRAFT
    n_col = iota((GRP * rows_p, rows_p), 1)
    new_ok = (lax.shift_right_logical(n_col, 2) == lax.shift_right_logical(block_row, 2)) & (
        n_col <= block_row
    )
    position = iota((GRP * rows_p, span), 1)

    def cached(slot, which, c, g):
        lanes = slice((c * KV_HERE + g) * HD, (c * KV_HERE + g + 1) * HD)
        return kv[pl.ds(slot * PPR, PPR), which, :, lanes].reshape(span, HD)

    def weigh(score, ok, new_score, new_ok):
        score = jnp.where(ok, score * factor, -1e30)
        new_score = jnp.where(new_ok, new_score * factor, -1e30)
        peak = jnp.maximum(
            jnp.max(score, axis=1, keepdims=True), jnp.max(new_score, axis=1, keepdims=True)
        )
        w = jnp.where(ok, jnp.exp(score - peak), 0.0)
        new_w = jnp.where(new_ok, jnp.exp(new_score - peak), 0.0)
        total = jnp.sum(w, axis=1, keepdims=True) + jnp.sum(new_w, axis=1, keepdims=True)
        return w.astype(BF16), new_w.astype(BF16), total

    def attend(c, g):
        for pr in range(R_DEV // 2):
            at = pr * rows_p
            slot = pr * 2
            limit = jnp.where(first, lengths[me * R_DEV + slot], lengths[me * R_DEV + slot + 1])
            both = [
                jnp.concatenate([cached(slot + a, which, c, g) for a in (0, 1)], axis=1)
                for which in (0, 1)
            ]
            tiles = []
            for h in range(GRP):
                p, i = divmod(g * GRP + h, PART_HEADS)
                r0 = p * n_rows + at
                tiles.append(rows[c, r0 : r0 + rows_p, i * HD : (i + 1) * HD])
            q = jnp.concatenate(tiles, axis=0)
            r0 = Q_PARTS * n_rows + at
            new_k = rows[c, r0 : r0 + rows_p, g * HD : (g + 1) * HD].astype(BF16)
            new_v = rows[c, r0 : r0 + rows_p, (KV_HERE + g) * HD : (KV_HERE + g + 1) * HD].astype(BF16)
            q2 = jnp.concatenate([jnp.where(first, q, 0.0), jnp.where(first, 0.0, q)], axis=1)
            w, new_w, total = weigh(
                dot_t(q2.astype(BF16), both[0]), position < limit, dot_t(q.astype(BF16), new_k), new_ok
            )
            out = dot(w, both[1])
            out = jnp.where(first, out[:, :HD], out[:, HD:]) + dot(new_w, new_v)
            res[c, g * GRP : (g + 1) * GRP, at : at + rows_p, :] = (out / total).reshape(
                GRP, rows_p, HD
            )

    v_rows = GRP * DRAFT
    v_row = iota((v_rows, 4 * DRAFT), 0)
    v_col = iota((v_rows, 4 * DRAFT), 1)
    v_position = iota((v_rows, span), 1)

    def attend_visitor(c, visitor):
        v = visitor.astype(F32)
        tail = v[:, PART_W:]
        new_k = tail.astype(BF16)
        new_v = jnp.concatenate([tail[2 * DRAFT :], tail[: 2 * DRAFT]], axis=0).astype(BF16)
        ok = v_position < lengths[me * R_DEV + my_slot]
        outs = []
        for g in range(KV_HERE):
            q = jnp.concatenate(
                [v[g * 2 * DRAFT : (g + 1) * 2 * DRAFT, i * HD : (i + 1) * HD] for i in range(PART_HEADS)],
                axis=0,
            ).astype(BF16)
            seen = (small_div(v_col, DRAFT) == g) & (small_mod(v_col, DRAFT) <= small_mod(v_row, DRAFT))
            w, new_w, total = weigh(
                dot_t(q, cached(my_slot, 0, c, g)), ok, dot_t(q, new_k), seen
            )
            outs.append((dot(w, cached(my_slot, 1, c, g)) + dot(new_w, new_v)) / total)
        return jnp.concatenate(outs, axis=0).astype(BF16)

    def arrive(c):
        wait_recv(send, recv, send_sem, recv_sem, c)
        got = recv[c].reshape(n * block, PART_W)
        stack = jnp.concatenate([got[:, i * HD : (i + 1) * HD] for i in range(4)], axis=0)
        mine = jnp.concatenate(
            [dot(x_pick[:, : n * block], got), dot(x_pick[:, n * block :], stack)], axis=1
        ).astype(BF16)
        return mine, got

    def pack_back(c):
        flat_res = res[c].reshape(flat, HD).astype(BF16)
        for m in range(cap):
            partial[c, :, m * HD : (m + 1) * HD] = dot(back_pick[m], flat_res)

    def send_back(c, answer):
        for m in range(cap):
            lanes = slice(m * HD, (m + 1) * HD)
            total = partial[c, :, lanes] + dot(y_pick[m], answer)
            back[c, :, :, lanes] = total.astype(BF16).reshape(n, HEADS, HD)
        send_all(back, home, back_sem, home_sem, c)

    def finish(c):
        wait_recv(back, home, back_sem, home_sem, c)
        got = home[c].reshape(n * HEADS, cap * HD)
        total = sum(dot(out_pick[m], got[:, m * HD : (m + 1) * HD]) for m in range(cap)).astype(BF16)
        for h in range(HEADS):
            lanes = slice((c * HEADS + h) * HD, (c * HEADS + h + 1) * HD)
            out_ref[:, lanes] = total[h * n_rows : (h + 1) * n_rows]

    mine0, got = arrive(0)
    rows[0] = dot(unpack[...], got)
    kv_copy.wait()
    attend(0, 0)
    attend(0, 1)
    mine1, got = arrive(1)
    moving = Swap([mine0, mine1], xs, xr, xs_sem, xr_sem)
    rows[1] = dot(unpack[...], got)
    attend(1, 0)
    moving.step()
    attend(1, 1)
    visitors = moving.finish()
    answers = Swap([attend_visitor(c, visitors[c]) for c in range(CHUNKS)], ys, yr, ys_sem, yr_sem)
    pack_back(0)
    answers.step()
    pack_back(1)
    final = answers.finish()
    for c in range(CHUNKS):
        send_back(c, final[c])
    for c in range(CHUNKS):
        finish(c)
    for c in range(CHUNKS):
        wait_send(send, recv, send_sem, recv_sem, c)
        wait_send(back, home, back_sem, home_sem, c)


def on_device(
    kv_cache, draft_rows, cache_lengths, row_offsets, draft_order, pair_mask, moved_slots
):
    n = lax.axis_size("req")
    n_rows = draft_rows.shape[0]
    cap = n_rows // row_offsets.shape[0]
    block = -(-PARTS * cap // 16) * 16
    swaps = sum(values - 1 for _, values in digits_of(n))
    x_shape = (swaps, CHUNKS * 4 * DRAFT, PART_W + HD)
    y_shape = (swaps, CHUNKS * HEADS * DRAFT, HD)
    vmem, smem = pltpu.VMEM, pltpu.SMEM
    dma = pltpu.SemaphoreType.DMA
    return pl.pallas_call(
        functools.partial(kernel, n, cap),
        out_shape=jax.ShapeDtypeStruct((n_rows, QW), BF16),
        in_specs=[pl.BlockSpec(memory_space=smem)] * 3
        + [pl.BlockSpec(memory_space=vmem)] * 3
        + [pl.BlockSpec(memory_space=pl.ANY)],
        out_specs=pl.BlockSpec(memory_space=vmem),
        scratch_shapes=[
            vmem(kv_cache.shape, BF16),
            vmem((CHUNKS, n, block, PART_W), BF16),
            vmem((CHUNKS, n, block, PART_W), BF16),
            vmem((CHUNKS, PARTS * n_rows, PART_W), F32),
            vmem((CHUNKS, HEADS, n_rows, HD), F32),
            vmem((CHUNKS, n * HEADS, cap * HD), F32),
            vmem((CHUNKS, n, HEADS, cap * HD), BF16),
            vmem((CHUNKS, n, HEADS, cap * HD), BF16),
            vmem(x_shape, BF16),
            vmem(x_shape, BF16),
            vmem(y_shape, BF16),
            vmem(y_shape, BF16),
            vmem((PARTS * n_rows, n * block), BF16),
            vmem((4 * DRAFT, 5 * n * block), BF16),
            vmem((cap, n * HEADS, HEADS * n_rows), BF16),
            vmem((cap, n * HEADS, HEADS * DRAFT), BF16),
            vmem((cap, HEADS * n_rows, n * HEADS), BF16),
            dma,
            dma((CHUNKS, n)), dma((CHUNKS, n)), dma((CHUNKS, n)), dma((CHUNKS, n)),
            dma((swaps,)), dma((swaps,)), dma((swaps,)), dma((swaps,)),
        ],
        compiler_params=pltpu.CompilerParams(
            collective_id=0, has_side_effects=True, vmem_limit_bytes=56 * 1024 * 1024
        ),
    )(
        cache_lengths, pair_mask, moved_slots, draft_order.reshape(1, n_rows),
        row_offsets.reshape(1, row_offsets.shape[0]), draft_rows, kv_cache,
    )


def solution(mesh):
    in_specs = (
        P(("groups", "req"), None, None, None),
        P(("groups", "req"), None),
        P("groups"),
        P("groups"),
        P(("groups", "req")),
        P("groups"),
        P("groups"),
    )
    out_specs = P(("groups", "req"), None)
    return jax.shard_map(
        on_device, mesh=mesh, in_specs=in_specs, out_specs=out_specs, check_vma=False
    )
```

```python
import functools

import jax
import jax.numpy as jnp
from jax import lax
from jax.experimental import pallas as pl
from jax.experimental.pallas import tpu as pltpu
from jax.sharding import PartitionSpec as P

HD = 128
DRAFT = 4
PAGE = 128
R_DEV = 12
PPR = 3
QW = 4096
KVW = 512
GRP = 8
CHUNKS = 2
HEADS = QW // HD // CHUNKS
KV_HERE = KVW // HD // CHUNKS
PARTS = 5
PART_W = (QW + 2 * KVW) // CHUNKS // PARTS
Q_PARTS = HEADS * HD // PART_W
PART_HEADS = PART_W // HD
F32 = jnp.float32
BF16 = jnp.bfloat16
MESH = pl.DeviceIdType.MESH


def iota(shape, dim):
    return lax.broadcasted_iota(jnp.int32, shape, dim)


def small_div(x, c):
    return x if c == 1 else lax.shift_right_logical(x * (65536 // c + 1), 16)


def small_mod(x, c):
    return x - small_div(x, c) * c


def wrap(x, n):
    x = jnp.where(x < 0, x + n, x)
    return jnp.where(x >= n, x - n, x)


def lane_sum(hit, value):
    return jnp.sum(jnp.where(hit, value, 0).astype(F32), axis=1, keepdims=True).astype(jnp.int32)


def row_sum(hit, value):
    return jnp.sum(jnp.where(hit, value, 0).astype(F32), axis=0, keepdims=True).astype(jnp.int32)


def pick(columns, width):
    return (iota((columns.shape[0], width), 1) == columns).astype(F32).astype(BF16)


def dot(a, b):
    return jnp.dot(a, b, preferred_element_type=F32)


def dot_t(a, b):
    return lax.dot_general(a, b, (((1,), (1,)), ((), ())), preferred_element_type=F32)


def flip(device, delta):
    bit = 0
    out = device
    while delta >> bit:
        if (delta >> bit) & 1:
            out = out + (1 << bit) * (1 - 2 * ((device // (1 << bit)) % 2))
        bit += 1
    return out


def digits_of(n):
    bits = n.bit_length() - 1
    return [(b, 1 << min(2, bits - b)) for b in range(0, bits, 2)]


def kernel(
    n, cap, lengths, mask, moved, order_ref, off_ref, draft_ref, kv_hbm, out_ref,
    kv, send, recv, rows, res, partial, back, home, xs, xr, ys, yr,
    unpack, x_pick, back_pick, y_pick, out_pick,
    kv_sem, send_sem, recv_sem, back_sem, home_sem, xs_sem, xr_sem, ys_sem, yr_sem,
):
    me = lax.axis_index("req")
    n_rows = order_ref.shape[1]
    block = send.shape[2]
    n_off = off_ref.shape[1]
    digits = digits_of(n)

    kv_copy = pltpu.make_async_copy(kv_hbm, kv, kv_sem)
    kv_copy.start()

    bits = n.bit_length() - 1
    turn = [(1 << b) * (1 - 2 * ((me // (1 << b)) % 2)) for b in range(bits)]

    def peer_of(i):
        place = (i + me % 2) % (n - 1) + 1
        peer = me
        for b in range(bits):
            peer = peer + turn[b] * ((place // (1 << (bits - 1 - b))) % 2)
        return peer

    barrier = pltpu.get_barrier_semaphore()

    def greet(i, carry):
        pl.semaphore_signal(barrier, inc=1, device_id={"req": peer_of(i)}, device_id_type=MESH)
        return carry

    lax.fori_loop(0, n - 1, greet, 0)

    order = order_ref[...]
    off = off_ref[...]
    order_col = lane_sum(iota((n_rows, n_rows), 0) == iota((n_rows, n_rows), 1), order)
    off_of_row = lane_sum(iota((n_rows, n_off), 1) == small_div(order_col, cap), off)
    owner = wrap(me - off_of_row, n)
    place = small_mod(order_col, cap)
    wide = PARTS * n_rows
    col = iota((1, wide), 1)
    target = owner * block + place
    target = row_sum(iota((n_rows, wide), 0) == small_mod(col, n_rows), target)
    target = target + small_div(col, n_rows) * cap
    pack = (iota((n * block, wide), 0) == target).astype(F32).astype(BF16)

    def exchange(shape_send, shape_recv, s_sem, r_sem, c, peer):
        return pltpu.make_async_remote_copy(
            src_ref=shape_send.at[c, peer], dst_ref=shape_recv.at[c, me],
            send_sem=s_sem.at[c, peer], recv_sem=r_sem.at[c, me],
            device_id={"req": peer}, device_id_type=MESH,
        )

    def send_all(s_ref, r_ref, s_sem, r_sem, c, lo=0, hi=n - 1):
        def body(i, carry):
            exchange(s_ref, r_ref, s_sem, r_sem, c, peer_of(i)).start()
            return carry

        lax.fori_loop(lo, hi, body, 0)
        if lo == 0:
            r_ref[c, me] = s_ref[c, me]

    def wait_recv(s_ref, r_ref, s_sem, r_sem, c):
        def body(i, carry):
            src = peer_of(i)
            pltpu.make_async_remote_copy(
                src_ref=s_ref.at[c, src], dst_ref=r_ref.at[c, src],
                send_sem=s_sem.at[c, src], recv_sem=r_sem.at[c, src],
                device_id={"req": src}, device_id_type=MESH,
            ).wait_recv()
            return carry

        lax.fori_loop(0, n - 1, body, 0)

    def wait_send(s_ref, r_ref, s_sem, r_sem, c):
        def body(i, carry):
            exchange(s_ref, r_ref, s_sem, r_sem, c, peer_of(i)).wait_send()
            return carry

        lax.fori_loop(0, n - 1, body, 0)

    for c in range(CHUNKS):
        q0 = c * HEADS * HD
        kw = KV_HERE * HD
        keys = draft_ref[:, QW + c * kw : QW + (c + 1) * kw]
        vals = draft_ref[:, QW + KVW + c * kw : QW + KVW + (c + 1) * kw]
        parts = [draft_ref[:, q0 + p * PART_W : q0 + (p + 1) * PART_W] for p in range(Q_PARTS)]
        stacked = jnp.concatenate(parts + [jnp.concatenate([keys, vals], axis=1)], axis=0)
        send[c] = dot(pack, stacked).astype(BF16).reshape(n, block, PART_W)
        if c == 0:
            pl.semaphore_wait(barrier, n - 1)
        send_all(send, recv, send_sem, recv_sem, c)

    my_slot = moved[me]
    pair = mask[0]
    r_col = iota((wide, 1), 0)
    k_col = small_mod(r_col, n_rows)
    off_col = lane_sum(iota((wide, n_off), 1) == small_div(k_col, cap), off)
    source = wrap(me + off_col, n)
    from_col = source * block + small_div(r_col, n_rows) * cap + small_mod(k_col, cap)
    unpack[...] = pick(from_col, n * block)
    x_row = iota((4 * DRAFT, 1), 0)
    x_draft = small_mod(x_row, DRAFT)
    x_k = my_slot * DRAFT + x_draft
    x_off = lane_sum(iota((4 * DRAFT, n_off), 1) == small_div(x_k, cap), off)
    x_from = wrap(me + x_off, n) * block + small_mod(x_k, cap)
    x_tile = small_div(x_row, DRAFT)
    x_pick[:, : n * block] = pick(x_from + x_tile * cap, n * block)
    for i in range(4):
        x_pick[:, (1 + i) * n * block : (2 + i) * n * block] = pick(
            jnp.where(x_tile == i, x_from + Q_PARTS * cap, -1), n * block
        )
    flat = HEADS * n_rows
    p_row = iota((n * HEADS, 1), 0)
    p_peer = small_div(p_row, HEADS)
    p_head = small_mod(p_row, HEADS)
    p_index = lane_sum(p_peer == wrap(me + off, n), iota((1, n_off), 1) + 1) - 1
    y_base = (
        small_div(p_head, GRP) * GRP * DRAFT
        + small_mod(p_head, PART_HEADS) * 2 * DRAFT
        + small_mod(small_div(p_head, PART_HEADS), 2) * DRAFT
    )
    for m in range(cap):
        p_k = p_index * cap + m
        p_moved = lax.shift_right_arithmetic(p_k, 2) == my_slot
        stays = (p_index >= 0) & jnp.logical_not(p_moved)
        back_pick[m] = pick(jnp.where(stays, p_head * n_rows + p_k, -1), flat)
        y_pick[m] = pick(jnp.where(p_moved, y_base + p_k - my_slot * DRAFT, -1), HEADS * DRAFT)
    f_row = iota((flat, 1), 0)
    j_hit = iota((flat, n_rows), 1) == small_mod(f_row, n_rows)
    eye = iota((n_rows, n_rows), 0) == iota((n_rows, n_rows), 1)
    out_from = lane_sum(j_hit, row_sum(eye, owner)) * HEADS + small_div(f_row, n_rows)
    out_place = lane_sum(j_hit, row_sum(eye, place))
    for m in range(cap):
        out_pick[m] = pick(jnp.where(out_place == m, out_from, -1), n * HEADS)

    class Swap:
        def __init__(self, cur, s_ref, r_ref, s_sem, r_sem, c):
            self.cur, self.refs, self.c = cur, (s_ref, r_ref, s_sem, r_sem), c
            self.slot, self.todo = 0, list(digits)
            self.start()

        def start(self):
            s_ref, r_ref, s_sem, r_sem = self.refs
            shift, values = self.todo[0]
            c, slot = self.c, self.slot
            s_ref[c, slot] = self.cur
            self.copies = [
                pltpu.make_async_remote_copy(
                    src_ref=s_ref.at[c, slot], dst_ref=r_ref.at[c, slot + delta - 1],
                    send_sem=s_sem.at[c, slot + delta - 1],
                    recv_sem=r_sem.at[c, slot + delta - 1],
                    device_id={"req": flip(me, delta << shift)}, device_id_type=MESH,
                )
                for delta in range(1, values)
            ]
            for copy in self.copies:
                copy.start()

        def receive(self):
            r_ref = self.refs[1]
            shift, values = self.todo.pop(0)
            digit = jnp.bitwise_and(jnp.right_shift(pair, shift), values - 1)
            for delta in range(1, values):
                self.copies[delta - 1].wait()
                self.cur = jnp.where(digit == delta, r_ref[self.c, self.slot + delta - 1], self.cur)
            self.slot += values - 1

        def step(self):
            self.receive()
            if self.todo:
                self.start()

        def finish(self):
            while self.todo:
                self.step()
            return self.cur

    rows_p = 2 * DRAFT
    span = PPR * PAGE
    factor = 1.0 / jnp.sqrt(F32(HD))
    block_row = small_mod(iota((GRP * rows_p, 1), 0), rows_p)
    first = block_row < DRAFT
    n_col = iota((GRP * rows_p, rows_p), 1)
    new_ok = (lax.shift_right_logical(n_col, 2) == lax.shift_right_logical(block_row, 2)) & (
        n_col <= block_row
    )
    position = iota((GRP * rows_p, span), 1)

    def cached(slot, which, c, g):
        lanes = slice((c * KV_HERE + g) * HD, (c * KV_HERE + g + 1) * HD)
        return kv[pl.ds(slot * PPR, PPR), which, :, lanes].reshape(span, HD)

    def weigh(score, ok, new_score, new_ok):
        score = jnp.where(ok, score * factor, -1e30)
        new_score = jnp.where(new_ok, new_score * factor, -1e30)
        peak = jnp.maximum(
            jnp.max(score, axis=1, keepdims=True), jnp.max(new_score, axis=1, keepdims=True)
        )
        w = jnp.where(ok, jnp.exp(score - peak), 0.0)
        new_w = jnp.where(new_ok, jnp.exp(new_score - peak), 0.0)
        total = jnp.sum(w, axis=1, keepdims=True) + jnp.sum(new_w, axis=1, keepdims=True)
        return w.astype(BF16), new_w.astype(BF16), total

    def attend(c, g):
        for pr in range(R_DEV // 2):
            at = pr * rows_p
            slot = pr * 2
            limit = jnp.where(first, lengths[me * R_DEV + slot], lengths[me * R_DEV + slot + 1])
            both = [
                jnp.concatenate([cached(slot + a, which, c, g) for a in (0, 1)], axis=1)
                for which in (0, 1)
            ]
            tiles = []
            for h in range(GRP):
                p, i = divmod(g * GRP + h, PART_HEADS)
                r0 = p * n_rows + at
                tiles.append(rows[c, r0 : r0 + rows_p, i * HD : (i + 1) * HD])
            q = jnp.concatenate(tiles, axis=0)
            r0 = Q_PARTS * n_rows + at
            new_k = rows[c, r0 : r0 + rows_p, g * HD : (g + 1) * HD].astype(BF16)
            new_v = rows[c, r0 : r0 + rows_p, (KV_HERE + g) * HD : (KV_HERE + g + 1) * HD].astype(BF16)
            q2 = jnp.concatenate([jnp.where(first, q, 0.0), jnp.where(first, 0.0, q)], axis=1)
            w, new_w, total = weigh(
                dot_t(q2.astype(BF16), both[0]), position < limit, dot_t(q.astype(BF16), new_k), new_ok
            )
            out = dot(w, both[1])
            out = jnp.where(first, out[:, :HD], out[:, HD:]) + dot(new_w, new_v)
            res[c, g * GRP : (g + 1) * GRP, at : at + rows_p, :] = (out / total).reshape(
                GRP, rows_p, HD
            )

    v_rows = GRP * DRAFT
    v_row = iota((v_rows, 4 * DRAFT), 0)
    v_col = iota((v_rows, 4 * DRAFT), 1)
    v_position = iota((v_rows, span), 1)

    def attend_visitor(c, visitor):
        v = visitor.astype(F32)
        tail = v[:, PART_W:]
        new_k = tail.astype(BF16)
        new_v = jnp.concatenate([tail[2 * DRAFT :], tail[: 2 * DRAFT]], axis=0).astype(BF16)
        ok = v_position < lengths[me * R_DEV + my_slot]
        outs = []
        for g in range(KV_HERE):
            q = jnp.concatenate(
                [v[g * 2 * DRAFT : (g + 1) * 2 * DRAFT, i * HD : (i + 1) * HD] for i in range(PART_HEADS)],
                axis=0,
            ).astype(BF16)
            seen = (small_div(v_col, DRAFT) == g) & (small_mod(v_col, DRAFT) <= small_mod(v_row, DRAFT))
            w, new_w, total = weigh(
                dot_t(q, cached(my_slot, 0, c, g)), ok, dot_t(q, new_k), seen
            )
            outs.append((dot(w, cached(my_slot, 1, c, g)) + dot(new_w, new_v)) / total)
        return jnp.concatenate(outs, axis=0).astype(BF16)

    def arrive(c):
        wait_recv(send, recv, send_sem, recv_sem, c)
        got = recv[c].reshape(n * block, PART_W)
        stack = jnp.concatenate([got[:, i * HD : (i + 1) * HD] for i in range(4)], axis=0)
        mine = jnp.concatenate(
            [dot(x_pick[:, : n * block], got), dot(x_pick[:, n * block :], stack)], axis=1
        ).astype(BF16)
        x_swap = Swap(mine, xs, xr, xs_sem, xr_sem, c)
        rows[c] = dot(unpack[...], got)
        return x_swap

    def pack_back(c):
        flat_res = res[c].reshape(flat, HD).astype(BF16)
        for m in range(cap):
            partial[c, :, m * HD : (m + 1) * HD] = dot(back_pick[m], flat_res)

    def send_answers(c, lo=0, hi=n - 1):
        send_all(back, home, back_sem, home_sem, c, lo, hi)

    def send_back(c, answer):
        for m in range(cap):
            lanes = slice(m * HD, (m + 1) * HD)
            total = partial[c, :, lanes] + dot(y_pick[m], answer)
            back[c, :, :, lanes] = total.astype(BF16).reshape(n, HEADS, HD)

    def finish(c):
        wait_recv(back, home, back_sem, home_sem, c)
        got = home[c].reshape(n * HEADS, cap * HD)
        total = sum(dot(out_pick[m], got[:, m * HD : (m + 1) * HD]) for m in range(cap)).astype(BF16)
        for h in range(HEADS):
            lanes = slice((c * HEADS + h) * HD, (c * HEADS + h + 1) * HD)
            out_ref[:, lanes] = total[h * n_rows : (h + 1) * n_rows]

    x0 = arrive(0)
    kv_copy.wait()
    attend(0, 0)
    x0.step()
    attend(0, 1)
    x1 = arrive(1)
    y0 = Swap(attend_visitor(0, x0.finish()), ys, yr, ys_sem, yr_sem, 0)
    attend(1, 0)
    x1.step()
    y0.step()
    attend(1, 1)
    pack_back(0)
    send_back(0, y0.finish())
    y1 = Swap(attend_visitor(1, x1.finish()), ys, yr, ys_sem, yr_sem, 1)
    send_answers(0, 0, n // 2)
    pack_back(1)
    y1.step()
    send_answers(0, n // 2)
    send_back(1, y1.finish())
    send_answers(1)
    finish(0)
    finish(1)
    for c in range(CHUNKS):
        wait_send(send, recv, send_sem, recv_sem, c)
        wait_send(back, home, back_sem, home_sem, c)


def on_device(
    kv_cache, draft_rows, cache_lengths, row_offsets, draft_order, pair_mask, moved_slots
):
    n = lax.axis_size("req")
    n_rows = draft_rows.shape[0]
    cap = n_rows // row_offsets.shape[0]
    block = -(-PARTS * cap // 16) * 16
    swaps = sum(values - 1 for _, values in digits_of(n))
    x_shape = (CHUNKS, swaps, 4 * DRAFT, PART_W + HD)
    y_shape = (CHUNKS, swaps, HEADS * DRAFT, HD)
    vmem, smem = pltpu.VMEM, pltpu.SMEM
    dma = pltpu.SemaphoreType.DMA
    return pl.pallas_call(
        functools.partial(kernel, n, cap),
        out_shape=jax.ShapeDtypeStruct((n_rows, QW), BF16),
        in_specs=[pl.BlockSpec(memory_space=smem)] * 3
        + [pl.BlockSpec(memory_space=vmem)] * 3
        + [pl.BlockSpec(memory_space=pl.ANY)],
        out_specs=pl.BlockSpec(memory_space=vmem),
        scratch_shapes=[
            vmem(kv_cache.shape, BF16),
            vmem((CHUNKS, n, block, PART_W), BF16),
            vmem((CHUNKS, n, block, PART_W), BF16),
            vmem((CHUNKS, PARTS * n_rows, PART_W), F32),
            vmem((CHUNKS, HEADS, n_rows, HD), F32),
            vmem((CHUNKS, n * HEADS, cap * HD), F32),
            vmem((CHUNKS, n, HEADS, cap * HD), BF16),
            vmem((CHUNKS, n, HEADS, cap * HD), BF16),
            vmem(x_shape, BF16),
            vmem(x_shape, BF16),
            vmem(y_shape, BF16),
            vmem(y_shape, BF16),
            vmem((PARTS * n_rows, n * block), BF16),
            vmem((4 * DRAFT, 5 * n * block), BF16),
            vmem((cap, n * HEADS, HEADS * n_rows), BF16),
            vmem((cap, n * HEADS, HEADS * DRAFT), BF16),
            vmem((cap, HEADS * n_rows, n * HEADS), BF16),
            dma,
            dma((CHUNKS, n)), dma((CHUNKS, n)), dma((CHUNKS, n)), dma((CHUNKS, n)),
            dma((CHUNKS, swaps)), dma((CHUNKS, swaps)), dma((CHUNKS, swaps)), dma((CHUNKS, swaps)),
        ],
        compiler_params=pltpu.CompilerParams(
            collective_id=0, has_side_effects=True, vmem_limit_bytes=56 * 1024 * 1024
        ),
    )(
        cache_lengths, pair_mask, moved_slots, draft_order.reshape(1, n_rows),
        row_offsets.reshape(1, row_offsets.shape[0]), draft_rows, kv_cache,
    )


def solution(mesh):
    in_specs = (
        P(("groups", "req"), None, None, None),
        P(("groups", "req"), None),
        P("groups"),
        P("groups"),
        P(("groups", "req")),
        P("groups"),
        P("groups"),
    )
    out_specs = P(("groups", "req"), None)
    return jax.shard_map(
        on_device, mesh=mesh, in_specs=in_specs, out_specs=out_specs, check_vma=False
    )
```

```python
import functools

import jax
import jax.numpy as jnp
from jax import lax
from jax.experimental import pallas as pl
from jax.experimental.pallas import tpu as pltpu
from jax.sharding import PartitionSpec as P

HD = 128
DRAFT = 4
PAGE = 128
R_DEV = 12
PPR = 3
QW = 4096
KVW = 512
GRP = 8
CHUNKS = 2
HEADS = QW // HD // CHUNKS
KV_HERE = KVW // HD // CHUNKS
PARTS = 5
PART_W = (QW + 2 * KVW) // CHUNKS // PARTS
Q_PARTS = HEADS * HD // PART_W
PART_HEADS = PART_W // HD
F32 = jnp.float32
BF16 = jnp.bfloat16
MESH = pl.DeviceIdType.MESH


def iota(shape, dim):
    return lax.broadcasted_iota(jnp.int32, shape, dim)


def small_div(x, c):
    return x if c == 1 else lax.shift_right_logical(x * (65536 // c + 1), 16)


def small_mod(x, c):
    return x - small_div(x, c) * c


def wrap(x, n):
    x = jnp.where(x < 0, x + n, x)
    return jnp.where(x >= n, x - n, x)


def lane_sum(hit, value):
    return jnp.sum(jnp.where(hit, value, 0).astype(F32), axis=1, keepdims=True).astype(jnp.int32)


def row_sum(hit, value):
    return jnp.sum(jnp.where(hit, value, 0).astype(F32), axis=0, keepdims=True).astype(jnp.int32)


def pick(columns, width):
    return (iota((columns.shape[0], width), 1) == columns).astype(F32).astype(BF16)


def dot(a, b):
    return jnp.dot(a, b, preferred_element_type=F32)


def dot_t(a, b):
    return lax.dot_general(a, b, (((1,), (1,)), ((), ())), preferred_element_type=F32)


def flip(device, delta):
    bit = 0
    out = device
    while delta >> bit:
        if (delta >> bit) & 1:
            out = out + (1 << bit) * (1 - 2 * ((device // (1 << bit)) % 2))
        bit += 1
    return out


def digits_of(n):
    bits = n.bit_length() - 1
    return [(b, 1 << min(2, bits - b)) for b in range(0, bits, 2)]


def kernel(
    n, cap, lengths, mask, moved, order_ref, off_ref, draft_ref, kv_hbm, out_ref,
    kv, send, recv, rows, res, partial, back, home, xs, xr, ys, yr,
    unpack, x_pick, back_pick, y_pick, out_pick, keys_t,
    kv_sem, send_sem, recv_sem, back_sem, home_sem, xs_sem, xr_sem, ys_sem, yr_sem,
):
    me = lax.axis_index("req")
    n_rows = order_ref.shape[1]
    block = send.shape[2]
    n_off = off_ref.shape[1]
    digits = digits_of(n)

    kv_copy = pltpu.make_async_copy(kv_hbm, kv, kv_sem)
    kv_copy.start()

    def peer_of(i):
        step = (i + n // 2 - 1) % (n - 1) + 1
        return (me + step) % n

    barrier = pltpu.get_barrier_semaphore()

    def greet(i, carry):
        pl.semaphore_signal(barrier, inc=1, device_id={"req": peer_of(i)}, device_id_type=MESH)
        return carry

    lax.fori_loop(0, n - 1, greet, 0)

    order = order_ref[...]
    off = off_ref[...]
    order_col = lane_sum(iota((n_rows, n_rows), 0) == iota((n_rows, n_rows), 1), order)
    off_of_row = lane_sum(iota((n_rows, n_off), 1) == small_div(order_col, cap), off)
    owner = wrap(me - off_of_row, n)
    place = small_mod(order_col, cap)
    wide = PARTS * n_rows
    col = iota((1, wide), 1)
    target = owner * block + place
    target = row_sum(iota((n_rows, wide), 0) == small_mod(col, n_rows), target)
    target = target + small_div(col, n_rows) * cap
    pack = (iota((n * block, wide), 0) == target).astype(F32).astype(BF16)

    def exchange(shape_send, shape_recv, s_sem, r_sem, c, peer):
        return pltpu.make_async_remote_copy(
            src_ref=shape_send.at[c, peer], dst_ref=shape_recv.at[c, me],
            send_sem=s_sem.at[c, peer], recv_sem=r_sem.at[c, me],
            device_id={"req": peer}, device_id_type=MESH,
        )

    def send_all(s_ref, r_ref, s_sem, r_sem, c):
        def body(i, carry):
            exchange(s_ref, r_ref, s_sem, r_sem, c, peer_of(i)).start()
            return carry

        lax.fori_loop(0, n - 1, body, 0)
        r_ref[c, me] = s_ref[c, me]

    def wait_recv(s_ref, r_ref, s_sem, r_sem, c):
        def body(i, carry):
            src = peer_of(i)
            pltpu.make_async_remote_copy(
                src_ref=s_ref.at[c, src], dst_ref=r_ref.at[c, src],
                send_sem=s_sem.at[c, src], recv_sem=r_sem.at[c, src],
                device_id={"req": src}, device_id_type=MESH,
            ).wait_recv()
            return carry

        lax.fori_loop(0, n - 1, body, 0)

    def wait_send(s_ref, r_ref, s_sem, r_sem, c):
        def body(i, carry):
            exchange(s_ref, r_ref, s_sem, r_sem, c, peer_of(i)).wait_send()
            return carry

        lax.fori_loop(0, n - 1, body, 0)

    for c in range(CHUNKS):
        q0 = c * HEADS * HD
        kw = KV_HERE * HD
        keys = draft_ref[:, QW + c * kw : QW + (c + 1) * kw]
        vals = draft_ref[:, QW + KVW + c * kw : QW + KVW + (c + 1) * kw]
        parts = [draft_ref[:, q0 + p * PART_W : q0 + (p + 1) * PART_W] for p in range(Q_PARTS)]
        stacked = jnp.concatenate(parts + [jnp.concatenate([keys, vals], axis=1)], axis=0)
        send[c] = dot(pack, stacked).astype(BF16).reshape(n, block, PART_W)
        if c == 0:
            pl.semaphore_wait(barrier, n - 1)
        send_all(send, recv, send_sem, recv_sem, c)

    my_slot = moved[me]
    pair = mask[0]
    r_col = iota((wide, 1), 0)
    k_col = small_mod(r_col, n_rows)
    off_col = lane_sum(iota((wide, n_off), 1) == small_div(k_col, cap), off)
    source = wrap(me + off_col, n)
    from_col = source * block + small_div(r_col, n_rows) * cap + small_mod(k_col, cap)
    unpack[...] = pick(from_col, n * block)
    x_row = iota((4 * DRAFT, 1), 0)
    x_draft = small_mod(x_row, DRAFT)
    x_k = my_slot * DRAFT + x_draft
    x_off = lane_sum(iota((4 * DRAFT, n_off), 1) == small_div(x_k, cap), off)
    x_from = wrap(me + x_off, n) * block + small_mod(x_k, cap)
    x_tile = small_div(x_row, DRAFT)
    x_pick[:, : n * block] = pick(x_from + x_tile * cap, n * block)
    for i in range(4):
        x_pick[:, (1 + i) * n * block : (2 + i) * n * block] = pick(
            jnp.where(x_tile == i, x_from + Q_PARTS * cap, -1), n * block
        )
    flat = HEADS * n_rows
    p_row = iota((n * HEADS, 1), 0)
    p_peer = small_div(p_row, HEADS)
    p_head = small_mod(p_row, HEADS)
    p_index = lane_sum(p_peer == wrap(me + off, n), iota((1, n_off), 1) + 1) - 1
    y_base = (
        small_div(p_head, GRP) * GRP * DRAFT
        + small_mod(p_head, PART_HEADS) * 2 * DRAFT
        + small_mod(small_div(p_head, PART_HEADS), 2) * DRAFT
    )
    for m in range(cap):
        p_k = p_index * cap + m
        p_moved = lax.shift_right_arithmetic(p_k, 2) == my_slot
        stays = (p_index >= 0) & jnp.logical_not(p_moved)
        back_pick[m] = pick(jnp.where(stays, p_head * n_rows + p_k, -1), flat)
        y_pick[m] = pick(jnp.where(p_moved, y_base + p_k - my_slot * DRAFT, -1), HEADS * DRAFT)
    f_row = iota((flat, 1), 0)
    j_hit = iota((flat, n_rows), 1) == small_mod(f_row, n_rows)
    eye = iota((n_rows, n_rows), 0) == iota((n_rows, n_rows), 1)
    out_from = lane_sum(j_hit, row_sum(eye, owner)) * HEADS + small_div(f_row, n_rows)
    out_place = lane_sum(j_hit, row_sum(eye, place))
    for m in range(cap):
        out_pick[m] = pick(jnp.where(out_place == m, out_from, -1), n * HEADS)

    class Swap:
        def __init__(self, cur, s_ref, r_ref, s_sem, r_sem, c):
            self.cur, self.refs, self.c = cur, (s_ref, r_ref, s_sem, r_sem), c
            self.slot, self.todo = 0, list(digits)
            self.start()

        def start(self):
            s_ref, r_ref, s_sem, r_sem = self.refs
            shift, values = self.todo[0]
            c, slot = self.c, self.slot
            s_ref[c, slot] = self.cur
            self.copies = [
                pltpu.make_async_remote_copy(
                    src_ref=s_ref.at[c, slot], dst_ref=r_ref.at[c, slot + delta - 1],
                    send_sem=s_sem.at[c, slot + delta - 1],
                    recv_sem=r_sem.at[c, slot + delta - 1],
                    device_id={"req": flip(me, delta << shift)}, device_id_type=MESH,
                )
                for delta in range(1, values)
            ]
            for copy in self.copies:
                copy.start()

        def receive(self):
            r_ref = self.refs[1]
            shift, values = self.todo.pop(0)
            digit = jnp.bitwise_and(jnp.right_shift(pair, shift), values - 1)
            for delta in range(1, values):
                self.copies[delta - 1].wait()
                self.cur = jnp.where(digit == delta, r_ref[self.c, self.slot + delta - 1], self.cur)
            self.slot += values - 1

        def step(self):
            self.receive()
            if self.todo:
                self.start()

        def finish(self):
            while self.todo:
                self.step()
            return self.cur

    rows_p = 2 * DRAFT
    span = PPR * PAGE
    factor = 1.0 / jnp.sqrt(F32(HD))
    block_row = small_mod(iota((GRP * rows_p, 1), 0), rows_p)
    first = block_row < DRAFT
    n_col = iota((GRP * rows_p, rows_p), 1)
    new_ok = (lax.shift_right_logical(n_col, 2) == lax.shift_right_logical(block_row, 2)) & (
        n_col <= block_row
    )
    position = iota((GRP * rows_p, span), 1)

    def cached(slot, which, c, g):
        lanes = slice((c * KV_HERE + g) * HD, (c * KV_HERE + g + 1) * HD)
        return kv[pl.ds(slot * PPR, PPR), which, :, lanes].reshape(span, HD)

    def weigh(score, ok, new_score, new_ok):
        score = jnp.where(ok, score * factor, -1e30)
        new_score = jnp.where(new_ok, new_score * factor, -1e30)
        peak = jnp.maximum(
            jnp.max(score, axis=1, keepdims=True), jnp.max(new_score, axis=1, keepdims=True)
        )
        w = jnp.where(ok, jnp.exp(score - peak), 0.0)
        new_w = jnp.where(new_ok, jnp.exp(new_score - peak), 0.0)
        total = jnp.sum(w, axis=1, keepdims=True) + jnp.sum(new_w, axis=1, keepdims=True)
        return w.astype(BF16), new_w.astype(BF16), total

    def attend(c, g):
        for pr in range(R_DEV // 2):
            at = pr * rows_p
            slot = pr * 2
            limit = jnp.where(first, lengths[me * R_DEV + slot], lengths[me * R_DEV + slot + 1])
            values = jnp.concatenate([cached(slot + a, 1, c, g) for a in (0, 1)], axis=1)
            tiles = []
            for h in range(GRP):
                p, i = divmod(g * GRP + h, PART_HEADS)
                r0 = p * n_rows + at
                tiles.append(rows[c, r0 : r0 + rows_p, i * HD : (i + 1) * HD])
            q = jnp.concatenate(tiles, axis=0)
            r0 = Q_PARTS * n_rows + at
            new_k = rows[c, r0 : r0 + rows_p, g * HD : (g + 1) * HD].astype(BF16)
            new_v = rows[c, r0 : r0 + rows_p, (KV_HERE + g) * HD : (KV_HERE + g + 1) * HD].astype(BF16)
            q2 = jnp.concatenate([jnp.where(first, q, 0.0), jnp.where(first, 0.0, q)], axis=1)
            w, new_w, total = weigh(
                dot(q2.astype(BF16), keys_t[c, g, pr]), position < limit, dot_t(q.astype(BF16), new_k), new_ok
            )
            out = dot(w, values)
            out = jnp.where(first, out[:, :HD], out[:, HD:]) + dot(new_w, new_v)
            res[c, g * GRP : (g + 1) * GRP, at : at + rows_p, :] = (out / total).reshape(
                GRP, rows_p, HD
            )

    v_rows = GRP * DRAFT
    v_row = iota((v_rows, 4 * DRAFT), 0)
    v_col = iota((v_rows, 4 * DRAFT), 1)
    v_position = iota((v_rows, span), 1)

    def attend_visitor(c, visitor):
        v = visitor.astype(F32)
        tail = v[:, PART_W:]
        new_k = tail.astype(BF16)
        new_v = jnp.concatenate([tail[2 * DRAFT :], tail[: 2 * DRAFT]], axis=0).astype(BF16)
        ok = v_position < lengths[me * R_DEV + my_slot]
        outs = []
        for g in range(KV_HERE):
            q = jnp.concatenate(
                [v[g * 2 * DRAFT : (g + 1) * 2 * DRAFT, i * HD : (i + 1) * HD] for i in range(PART_HEADS)],
                axis=0,
            ).astype(BF16)
            seen = (small_div(v_col, DRAFT) == g) & (small_mod(v_col, DRAFT) <= small_mod(v_row, DRAFT))
            w, new_w, total = weigh(
                dot_t(q, cached(my_slot, 0, c, g)), ok, dot_t(q, new_k), seen
            )
            outs.append((dot(w, cached(my_slot, 1, c, g)) + dot(new_w, new_v)) / total)
        return jnp.concatenate(outs, axis=0).astype(BF16)

    def arrive(c):
        wait_recv(send, recv, send_sem, recv_sem, c)
        got = recv[c].reshape(n * block, PART_W)
        stack = jnp.concatenate([got[:, i * HD : (i + 1) * HD] for i in range(4)], axis=0)
        mine = jnp.concatenate(
            [dot(x_pick[:, : n * block], got), dot(x_pick[:, n * block :], stack)], axis=1
        ).astype(BF16)
        x_swap = Swap(mine, xs, xr, xs_sem, xr_sem, c)
        rows[c] = dot(unpack[...], got)
        return x_swap

    def pack_back(c):
        flat_res = res[c].reshape(flat, HD).astype(BF16)
        for m in range(cap):
            partial[c, :, m * HD : (m + 1) * HD] = dot(back_pick[m], flat_res)

    def send_back(c, answer):
        for m in range(cap):
            lanes = slice(m * HD, (m + 1) * HD)
            total = partial[c, :, lanes] + dot(y_pick[m], answer)
            back[c, :, :, lanes] = total.astype(BF16).reshape(n, HEADS, HD)
        send_all(back, home, back_sem, home_sem, c)

    def finish(c):
        wait_recv(back, home, back_sem, home_sem, c)
        got = home[c].reshape(n * HEADS, cap * HD)
        total = sum(dot(out_pick[m], got[:, m * HD : (m + 1) * HD]) for m in range(cap)).astype(BF16)
        for h in range(HEADS):
            lanes = slice((c * HEADS + h) * HD, (c * HEADS + h + 1) * HD)
            out_ref[:, lanes] = total[h * n_rows : (h + 1) * n_rows]

    kv_copy.wait()
    for c in range(CHUNKS):
        for g in range(KV_HERE):
            for pr in range(R_DEV // 2):
                keys_t[c, g, pr] = jnp.concatenate(
                    [cached(pr * 2 + a, 0, c, g) for a in (0, 1)], axis=1
                ).T
    x0 = arrive(0)
    attend(0, 0)
    x0.step()
    attend(0, 1)
    x1 = arrive(1)
    y0 = Swap(attend_visitor(0, x0.finish()), ys, yr, ys_sem, yr_sem, 0)
    attend(1, 0)
    x1.step()
    y0.step()
    attend(1, 1)
    pack_back(0)
    send_back(0, y0.finish())
    y1 = Swap(attend_visitor(1, x1.finish()), ys, yr, ys_sem, yr_sem, 1)
    pack_back(1)
    send_back(1, y1.finish())
    finish(0)
    finish(1)
    for c in range(CHUNKS):
        wait_send(send, recv, send_sem, recv_sem, c)
        wait_send(back, home, back_sem, home_sem, c)


def on_device(
    kv_cache, draft_rows, cache_lengths, row_offsets, draft_order, pair_mask, moved_slots
):
    n = lax.axis_size("req")
    n_rows = draft_rows.shape[0]
    cap = n_rows // row_offsets.shape[0]
    block = -(-PARTS * cap // 16) * 16
    swaps = sum(values - 1 for _, values in digits_of(n))
    x_shape = (CHUNKS, swaps, 4 * DRAFT, PART_W + HD)
    y_shape = (CHUNKS, swaps, HEADS * DRAFT, HD)
    vmem, smem = pltpu.VMEM, pltpu.SMEM
    dma = pltpu.SemaphoreType.DMA
    return pl.pallas_call(
        functools.partial(kernel, n, cap),
        out_shape=jax.ShapeDtypeStruct((n_rows, QW), BF16),
        in_specs=[pl.BlockSpec(memory_space=smem)] * 3
        + [pl.BlockSpec(memory_space=vmem)] * 3
        + [pl.BlockSpec(memory_space=pl.ANY)],
        out_specs=pl.BlockSpec(memory_space=vmem),
        scratch_shapes=[
            vmem(kv_cache.shape, BF16),
            vmem((CHUNKS, n, block, PART_W), BF16),
            vmem((CHUNKS, n, block, PART_W), BF16),
            vmem((CHUNKS, PARTS * n_rows, PART_W), F32),
            vmem((CHUNKS, HEADS, n_rows, HD), F32),
            vmem((CHUNKS, n * HEADS, cap * HD), F32),
            vmem((CHUNKS, n, HEADS, cap * HD), BF16),
            vmem((CHUNKS, n, HEADS, cap * HD), BF16),
            vmem(x_shape, BF16),
            vmem(x_shape, BF16),
            vmem(y_shape, BF16),
            vmem(y_shape, BF16),
            vmem((PARTS * n_rows, n * block), BF16),
            vmem((4 * DRAFT, 5 * n * block), BF16),
            vmem((cap, n * HEADS, HEADS * n_rows), BF16),
            vmem((cap, n * HEADS, HEADS * DRAFT), BF16),
            vmem((cap, HEADS * n_rows, n * HEADS), BF16),
            vmem((CHUNKS, KV_HERE, R_DEV // 2, 2 * HD, PPR * PAGE), BF16),
            dma,
            dma((CHUNKS, n)), dma((CHUNKS, n)), dma((CHUNKS, n)), dma((CHUNKS, n)),
            dma((CHUNKS, swaps)), dma((CHUNKS, swaps)), dma((CHUNKS, swaps)), dma((CHUNKS, swaps)),
        ],
        compiler_params=pltpu.CompilerParams(
            collective_id=0, has_side_effects=True, vmem_limit_bytes=56 * 1024 * 1024
        ),
    )(
        cache_lengths, pair_mask, moved_slots, draft_order.reshape(1, n_rows),
        row_offsets.reshape(1, row_offsets.shape[0]), draft_rows, kv_cache,
    )


def solution(mesh):
    in_specs = (
        P(("groups", "req"), None, None, None),
        P(("groups", "req"), None),
        P("groups"),
        P("groups"),
        P(("groups", "req")),
        P("groups"),
        P("groups"),
    )
    out_specs = P(("groups", "req"), None)
    return jax.shard_map(
        on_device, mesh=mesh, in_specs=in_specs, out_specs=out_specs, check_vma=False
    )
```

```python
import functools

import jax
import jax.numpy as jnp
from jax import lax
from jax.experimental import pallas as pl
from jax.experimental.pallas import tpu as pltpu
from jax.sharding import PartitionSpec as P

HD = 128
DRAFT = 4
PAGE = 128
R_DEV = 12
PPR = 3
QW = 4096
KVW = 512
GRP = 8
CHUNKS = 2
HEADS = QW // HD // CHUNKS
KV_HERE = KVW // HD // CHUNKS
PARTS = 5
PART_W = (QW + 2 * KVW) // CHUNKS // PARTS
Q_PARTS = HEADS * HD // PART_W
PART_HEADS = PART_W // HD
F32 = jnp.float32
BF16 = jnp.bfloat16
MESH = pl.DeviceIdType.MESH


def iota(shape, dim):
    return lax.broadcasted_iota(jnp.int32, shape, dim)


def small_div(x, c):
    return x if c == 1 else lax.shift_right_logical(x * (65536 // c + 1), 16)


def small_mod(x, c):
    return x - small_div(x, c) * c


def wrap(x, n):
    x = jnp.where(x < 0, x + n, x)
    return jnp.where(x >= n, x - n, x)


def lane_sum(hit, value):
    return jnp.sum(jnp.where(hit, value, 0).astype(F32), axis=1, keepdims=True).astype(jnp.int32)


def row_sum(hit, value):
    return jnp.sum(jnp.where(hit, value, 0).astype(F32), axis=0, keepdims=True).astype(jnp.int32)


def pick(columns, width):
    return (iota((columns.shape[0], width), 1) == columns).astype(F32).astype(BF16)


def dot(a, b):
    return jnp.dot(a, b, preferred_element_type=F32)


def dot_t(a, b):
    return lax.dot_general(a, b, (((1,), (1,)), ((), ())), preferred_element_type=F32)


def flip(device, delta):
    bit = 0
    out = device
    while delta >> bit:
        if (delta >> bit) & 1:
            out = out + (1 << bit) * (1 - 2 * ((device // (1 << bit)) % 2))
        bit += 1
    return out


def digits_of(n):
    bits = n.bit_length() - 1
    return [(b, 1 << min(2, bits - b)) for b in range(0, bits, 2)]


def kernel(
    n, cap, lengths, mask, moved, order_ref, off_ref, draft_ref, kv_hbm, out_ref,
    kv, send, recv, rows, res, partial, back, home, xs, xr, ys, yr,
    unpack, x_pick, back_pick, y_pick, out_pick, keys_t,
    kv_sem, send_sem, recv_sem, back_sem, home_sem, xs_sem, xr_sem, ys_sem, yr_sem,
):
    me = lax.axis_index("req")
    n_rows = order_ref.shape[1]
    block = send.shape[2]
    n_off = off_ref.shape[1]
    digits = digits_of(n)

    kv_copy = pltpu.make_async_copy(kv_hbm, kv, kv_sem)
    kv_copy.start()

    def peer_of(i):
        step = (i + n // 2 - 1) % (n - 1) + 1
        return (me + step) % n

    barrier = pltpu.get_barrier_semaphore()

    def greet(i, carry):
        pl.semaphore_signal(barrier, inc=1, device_id={"req": peer_of(i)}, device_id_type=MESH)
        return carry

    lax.fori_loop(0, n - 1, greet, 0)

    order = order_ref[...]
    off = off_ref[...]
    order_col = lane_sum(iota((n_rows, n_rows), 0) == iota((n_rows, n_rows), 1), order)
    off_of_row = lane_sum(iota((n_rows, n_off), 1) == small_div(order_col, cap), off)
    owner = wrap(me - off_of_row, n)
    place = small_mod(order_col, cap)
    wide = PARTS * n_rows
    col = iota((1, wide), 1)
    target = owner * block + place
    target = row_sum(iota((n_rows, wide), 0) == small_mod(col, n_rows), target)
    target = target + small_div(col, n_rows) * cap
    pack = (iota((n * block, wide), 0) == target).astype(F32).astype(BF16)

    def exchange(shape_send, shape_recv, s_sem, r_sem, c, peer):
        return pltpu.make_async_remote_copy(
            src_ref=shape_send.at[c, peer], dst_ref=shape_recv.at[c, me],
            send_sem=s_sem.at[c, peer], recv_sem=r_sem.at[c, me],
            device_id={"req": peer}, device_id_type=MESH,
        )

    def send_all(s_ref, r_ref, s_sem, r_sem, c, lo=0, hi=n - 1):
        def body(i, carry):
            exchange(s_ref, r_ref, s_sem, r_sem, c, peer_of(i)).start()
            return carry

        lax.fori_loop(lo, hi, body, 0)
        if lo == 0:
            r_ref[c, me] = s_ref[c, me]

    def wait_recv(s_ref, r_ref, s_sem, r_sem, c):
        def body(i, carry):
            src = peer_of(i)
            pltpu.make_async_remote_copy(
                src_ref=s_ref.at[c, src], dst_ref=r_ref.at[c, src],
                send_sem=s_sem.at[c, src], recv_sem=r_sem.at[c, src],
                device_id={"req": src}, device_id_type=MESH,
            ).wait_recv()
            return carry

        lax.fori_loop(0, n - 1, body, 0)

    def wait_send(s_ref, r_ref, s_sem, r_sem, c):
        def body(i, carry):
            exchange(s_ref, r_ref, s_sem, r_sem, c, peer_of(i)).wait_send()
            return carry

        lax.fori_loop(0, n - 1, body, 0)

    for c in range(CHUNKS):
        q0 = c * HEADS * HD
        kw = KV_HERE * HD
        keys = draft_ref[:, QW + c * kw : QW + (c + 1) * kw]
        vals = draft_ref[:, QW + KVW + c * kw : QW + KVW + (c + 1) * kw]
        parts = [draft_ref[:, q0 + p * PART_W : q0 + (p + 1) * PART_W] for p in range(Q_PARTS)]
        stacked = jnp.concatenate(parts + [jnp.concatenate([keys, vals], axis=1)], axis=0)
        send[c] = dot(pack, stacked).astype(BF16).reshape(n, block, PART_W)
        if c == 0:
            pl.semaphore_wait(barrier, n - 1)
        send_all(send, recv, send_sem, recv_sem, c, 0, n - 1 if c == 0 else n // 2)

    my_slot = moved[me]
    pair = mask[0]
    r_col = iota((wide, 1), 0)
    k_col = small_mod(r_col, n_rows)
    off_col = lane_sum(iota((wide, n_off), 1) == small_div(k_col, cap), off)
    source = wrap(me + off_col, n)
    from_col = source * block + small_div(r_col, n_rows) * cap + small_mod(k_col, cap)
    unpack[...] = pick(from_col, n * block)
    x_row = iota((4 * DRAFT, 1), 0)
    x_draft = small_mod(x_row, DRAFT)
    x_k = my_slot * DRAFT + x_draft
    x_off = lane_sum(iota((4 * DRAFT, n_off), 1) == small_div(x_k, cap), off)
    x_from = wrap(me + x_off, n) * block + small_mod(x_k, cap)
    x_tile = small_div(x_row, DRAFT)
    x_pick[:, : n * block] = pick(x_from + x_tile * cap, n * block)
    for i in range(4):
        x_pick[:, (1 + i) * n * block : (2 + i) * n * block] = pick(
            jnp.where(x_tile == i, x_from + Q_PARTS * cap, -1), n * block
        )
    flat = HEADS * n_rows
    p_row = iota((n * HEADS, 1), 0)
    p_peer = small_div(p_row, HEADS)
    p_head = small_mod(p_row, HEADS)
    p_index = lane_sum(p_peer == wrap(me + off, n), iota((1, n_off), 1) + 1) - 1
    y_base = (
        small_div(p_head, GRP) * GRP * DRAFT
        + small_mod(p_head, PART_HEADS) * 2 * DRAFT
        + small_mod(small_div(p_head, PART_HEADS), 2) * DRAFT
    )
    for m in range(cap):
        p_k = p_index * cap + m
        p_moved = lax.shift_right_arithmetic(p_k, 2) == my_slot
        stays = (p_index >= 0) & jnp.logical_not(p_moved)
        back_pick[m] = pick(jnp.where(stays, p_head * n_rows + p_k, -1), flat)
        y_pick[m] = pick(jnp.where(p_moved, y_base + p_k - my_slot * DRAFT, -1), HEADS * DRAFT)
    f_row = iota((flat, 1), 0)
    j_hit = iota((flat, n_rows), 1) == small_mod(f_row, n_rows)
    eye = iota((n_rows, n_rows), 0) == iota((n_rows, n_rows), 1)
    out_from = lane_sum(j_hit, row_sum(eye, owner)) * HEADS + small_div(f_row, n_rows)
    out_place = lane_sum(j_hit, row_sum(eye, place))
    for m in range(cap):
        out_pick[m] = pick(jnp.where(out_place == m, out_from, -1), n * HEADS)

    class Swap:
        def __init__(self, cur, s_ref, r_ref, s_sem, r_sem, c):
            self.cur, self.refs, self.c = cur, (s_ref, r_ref, s_sem, r_sem), c
            self.slot, self.todo = 0, list(digits)
            self.start()

        def start(self):
            s_ref, r_ref, s_sem, r_sem = self.refs
            shift, values = self.todo[0]
            c, slot = self.c, self.slot
            s_ref[c, slot] = self.cur
            self.copies = [
                pltpu.make_async_remote_copy(
                    src_ref=s_ref.at[c, slot], dst_ref=r_ref.at[c, slot + delta - 1],
                    send_sem=s_sem.at[c, slot + delta - 1],
                    recv_sem=r_sem.at[c, slot + delta - 1],
                    device_id={"req": flip(me, delta << shift)}, device_id_type=MESH,
                )
                for delta in range(1, values)
            ]
            for copy in self.copies:
                copy.start()

        def receive(self):
            r_ref = self.refs[1]
            shift, values = self.todo.pop(0)
            digit = jnp.bitwise_and(jnp.right_shift(pair, shift), values - 1)
            for delta in range(1, values):
                self.copies[delta - 1].wait()
                self.cur = jnp.where(digit == delta, r_ref[self.c, self.slot + delta - 1], self.cur)
            self.slot += values - 1

        def step(self):
            self.receive()
            if self.todo:
                self.start()

        def finish(self):
            while self.todo:
                self.step()
            return self.cur

    rows_p = 2 * DRAFT
    span = PPR * PAGE
    factor = 1.0 / jnp.sqrt(F32(HD))
    block_row = small_mod(iota((GRP * rows_p, 1), 0), rows_p)
    first = block_row < DRAFT
    n_col = iota((GRP * rows_p, rows_p), 1)
    new_ok = (lax.shift_right_logical(n_col, 2) == lax.shift_right_logical(block_row, 2)) & (
        n_col <= block_row
    )
    position = iota((GRP * rows_p, span), 1)

    def cached(slot, which, c, g):
        lanes = slice((c * KV_HERE + g) * HD, (c * KV_HERE + g + 1) * HD)
        return kv[pl.ds(slot * PPR, PPR), which, :, lanes].reshape(span, HD)

    def weigh(score, ok, new_score, new_ok):
        score = jnp.where(ok, score * factor, -1e30)
        new_score = jnp.where(new_ok, new_score * factor, -1e30)
        peak = jnp.maximum(
            jnp.max(score, axis=1, keepdims=True), jnp.max(new_score, axis=1, keepdims=True)
        )
        w = jnp.where(ok, jnp.exp(score - peak), 0.0)
        new_w = jnp.where(new_ok, jnp.exp(new_score - peak), 0.0)
        total = jnp.sum(w, axis=1, keepdims=True) + jnp.sum(new_w, axis=1, keepdims=True)
        return w.astype(BF16), new_w.astype(BF16), total

    def attend(c, g):
        for pr in range(R_DEV // 2):
            at = pr * rows_p
            slot = pr * 2
            limit = jnp.where(first, lengths[me * R_DEV + slot], lengths[me * R_DEV + slot + 1])
            values = jnp.concatenate([cached(slot + a, 1, c, g) for a in (0, 1)], axis=1)
            tiles = []
            for h in range(GRP):
                p, i = divmod(g * GRP + h, PART_HEADS)
                r0 = p * n_rows + at
                tiles.append(rows[c, r0 : r0 + rows_p, i * HD : (i + 1) * HD])
            q = jnp.concatenate(tiles, axis=0)
            r0 = Q_PARTS * n_rows + at
            new_k = rows[c, r0 : r0 + rows_p, g * HD : (g + 1) * HD].astype(BF16)
            new_v = rows[c, r0 : r0 + rows_p, (KV_HERE + g) * HD : (KV_HERE + g + 1) * HD].astype(BF16)
            q2 = jnp.concatenate([jnp.where(first, q, 0.0), jnp.where(first, 0.0, q)], axis=1)
            w, new_w, total = weigh(
                dot(q2.astype(BF16), keys_t[c, g, pr]), position < limit, dot_t(q.astype(BF16), new_k), new_ok
            )
            out = dot(w, values)
            out = jnp.where(first, out[:, :HD], out[:, HD:]) + dot(new_w, new_v)
            res[c, g * GRP : (g + 1) * GRP, at : at + rows_p, :] = (out / total).reshape(
                GRP, rows_p, HD
            )

    v_rows = GRP * DRAFT
    v_row = iota((v_rows, 4 * DRAFT), 0)
    v_col = iota((v_rows, 4 * DRAFT), 1)
    v_position = iota((v_rows, span), 1)

    def attend_visitor(c, visitor):
        v = visitor.astype(F32)
        tail = v[:, PART_W:]
        new_k = tail.astype(BF16)
        new_v = jnp.concatenate([tail[2 * DRAFT :], tail[: 2 * DRAFT]], axis=0).astype(BF16)
        ok = v_position < lengths[me * R_DEV + my_slot]
        outs = []
        for g in range(KV_HERE):
            q = jnp.concatenate(
                [v[g * 2 * DRAFT : (g + 1) * 2 * DRAFT, i * HD : (i + 1) * HD] for i in range(PART_HEADS)],
                axis=0,
            ).astype(BF16)
            seen = (small_div(v_col, DRAFT) == g) & (small_mod(v_col, DRAFT) <= small_mod(v_row, DRAFT))
            w, new_w, total = weigh(
                dot_t(q, cached(my_slot, 0, c, g)), ok, dot_t(q, new_k), seen
            )
            outs.append((dot(w, cached(my_slot, 1, c, g)) + dot(new_w, new_v)) / total)
        return jnp.concatenate(outs, axis=0).astype(BF16)

    def arrive(c):
        wait_recv(send, recv, send_sem, recv_sem, c)
        got = recv[c].reshape(n * block, PART_W)
        stack = jnp.concatenate([got[:, i * HD : (i + 1) * HD] for i in range(4)], axis=0)
        mine = jnp.concatenate(
            [dot(x_pick[:, : n * block], got), dot(x_pick[:, n * block :], stack)], axis=1
        ).astype(BF16)
        x_swap = Swap(mine, xs, xr, xs_sem, xr_sem, c)
        rows[c] = dot(unpack[...], got)
        return x_swap

    def pack_back(c):
        flat_res = res[c].reshape(flat, HD).astype(BF16)
        for m in range(cap):
            partial[c, :, m * HD : (m + 1) * HD] = dot(back_pick[m], flat_res)

    def send_back(c, answer):
        for m in range(cap):
            lanes = slice(m * HD, (m + 1) * HD)
            total = partial[c, :, lanes] + dot(y_pick[m], answer)
            back[c, :, :, lanes] = total.astype(BF16).reshape(n, HEADS, HD)
        send_all(back, home, back_sem, home_sem, c)

    def finish(c):
        wait_recv(back, home, back_sem, home_sem, c)
        got = home[c].reshape(n * HEADS, cap * HD)
        total = sum(dot(out_pick[m], got[:, m * HD : (m + 1) * HD]) for m in range(cap)).astype(BF16)
        for h in range(HEADS):
            lanes = slice((c * HEADS + h) * HD, (c * HEADS + h + 1) * HD)
            out_ref[:, lanes] = total[h * n_rows : (h + 1) * n_rows]

    kv_copy.wait()
    for c in range(CHUNKS):
        for g in range(KV_HERE):
            for pr in range(R_DEV // 2):
                keys_t[c, g, pr] = jnp.concatenate(
                    [cached(pr * 2 + a, 0, c, g) for a in (0, 1)], axis=1
                ).T
    x0 = arrive(0)
    attend(0, 0)
    x0.step()
    send_all(send, recv, send_sem, recv_sem, 1, n // 2)
    attend(0, 1)
    y0 = Swap(attend_visitor(0, x0.finish()), ys, yr, ys_sem, yr_sem, 0)
    pack_back(0)
    x1 = arrive(1)
    y0.step()
    attend(1, 0)
    x1.step()
    send_back(0, y0.finish())
    attend(1, 1)
    y1 = Swap(attend_visitor(1, x1.finish()), ys, yr, ys_sem, yr_sem, 1)
    pack_back(1)
    send_back(1, y1.finish())
    finish(0)
    finish(1)
    for c in range(CHUNKS):
        wait_send(send, recv, send_sem, recv_sem, c)
        wait_send(back, home, back_sem, home_sem, c)


def on_device(
    kv_cache, draft_rows, cache_lengths, row_offsets, draft_order, pair_mask, moved_slots
):
    n = lax.axis_size("req")
    n_rows = draft_rows.shape[0]
    cap = n_rows // row_offsets.shape[0]
    block = -(-PARTS * cap // 16) * 16
    swaps = sum(values - 1 for _, values in digits_of(n))
    x_shape = (CHUNKS, swaps, 4 * DRAFT, PART_W + HD)
    y_shape = (CHUNKS, swaps, HEADS * DRAFT, HD)
    vmem, smem = pltpu.VMEM, pltpu.SMEM
    dma = pltpu.SemaphoreType.DMA
    return pl.pallas_call(
        functools.partial(kernel, n, cap),
        out_shape=jax.ShapeDtypeStruct((n_rows, QW), BF16),
        in_specs=[pl.BlockSpec(memory_space=smem)] * 3
        + [pl.BlockSpec(memory_space=vmem)] * 3
        + [pl.BlockSpec(memory_space=pl.ANY)],
        out_specs=pl.BlockSpec(memory_space=vmem),
        scratch_shapes=[
            vmem(kv_cache.shape, BF16),
            vmem((CHUNKS, n, block, PART_W), BF16),
            vmem((CHUNKS, n, block, PART_W), BF16),
            vmem((CHUNKS, PARTS * n_rows, PART_W), F32),
            vmem((CHUNKS, HEADS, n_rows, HD), F32),
            vmem((CHUNKS, n * HEADS, cap * HD), F32),
            vmem((CHUNKS, n, HEADS, cap * HD), BF16),
            vmem((CHUNKS, n, HEADS, cap * HD), BF16),
            vmem(x_shape, BF16),
            vmem(x_shape, BF16),
            vmem(y_shape, BF16),
            vmem(y_shape, BF16),
            vmem((PARTS * n_rows, n * block), BF16),
            vmem((4 * DRAFT, 5 * n * block), BF16),
            vmem((cap, n * HEADS, HEADS * n_rows), BF16),
            vmem((cap, n * HEADS, HEADS * DRAFT), BF16),
            vmem((cap, HEADS * n_rows, n * HEADS), BF16),
            vmem((CHUNKS, KV_HERE, R_DEV // 2, 2 * HD, PPR * PAGE), BF16),
            dma,
            dma((CHUNKS, n)), dma((CHUNKS, n)), dma((CHUNKS, n)), dma((CHUNKS, n)),
            dma((CHUNKS, swaps)), dma((CHUNKS, swaps)), dma((CHUNKS, swaps)), dma((CHUNKS, swaps)),
        ],
        compiler_params=pltpu.CompilerParams(
            collective_id=0, has_side_effects=True, vmem_limit_bytes=56 * 1024 * 1024
        ),
    )(
        cache_lengths, pair_mask, moved_slots, draft_order.reshape(1, n_rows),
        row_offsets.reshape(1, row_offsets.shape[0]), draft_rows, kv_cache,
    )


def solution(mesh):
    in_specs = (
        P(("groups", "req"), None, None, None),
        P(("groups", "req"), None),
        P("groups"),
        P("groups"),
        P(("groups", "req")),
        P("groups"),
        P("groups"),
    )
    out_specs = P(("groups", "req"), None)
    return jax.shard_map(
        on_device, mesh=mesh, in_specs=in_specs, out_specs=out_specs, check_vma=False
    )
```
